256 devices in a mesh: tm: 8 (over z_hi, core), space: 32 (over z_lo, x, y).
Axes of the slice: x: 4, y: 4, z: 8 (z_hi: 4, z_lo: 2; z = z_hi * 2 + z_lo), core: 2. Of those that a mesh axis runs over, the one named last changes fastest.
Arguments:
- initial: float32 [4, 256, 16, 128], P(None, 'space'), may hold values from -6 to 6
- velocity: float32 [3, 256, 16, 128], P(None, 'space'), may hold values from -0.5 to 0.5
- diffusivity: float32 [256, 16, 128], P('space'), may hold values from 0.1 to 0.6
Outputs:
- final_nodes: float32 [8, 3, 4, 256, 16, 128], P('tm', None, None, 'space')
The draws below stay inside these ranges and needn't reach their ends.
All inputs are finite; a program needn't handle non-finite values.
Results may differ from the reference program's by a relative error of at most 0.00002.
Values sent between devices are 32-bit elements; how exact they have to be, the bound alone decides.
A program may use at most 64 MiB of HBM per device.

```python
import math
import jax
import jax.numpy as jnp

NTR = 4
NY = 16
NZ = 128
SWEEPS = 2
NT = 8
NX = 256


def block_levels(rng, shape, shards, smallest, largest):
    def one(axis_at, shards_of):
        steps = jax.random.uniform(jax.random.fold_in(jax.random.fold_in(rng, 6), axis_at), (shards_of,), jnp.float32, smallest / len(shards), largest / len(shards))
        return jnp.repeat(jnp.exp(steps), shape[axis_at] // shards_of).reshape((-1,) + (1,) * (len(shape) - axis_at - 1))

    factor_of = one(*shards[0])
    for cut in shards[1:]:
        factor_of = factor_of * one(*cut)
    return factor_of


def centred(own_key, extent, deviation, bound, cuts=(), dtype=jnp.bfloat16):
    array = deviation * jax.random.normal(own_key, extent, jnp.float32)
    if cuts:
        array = array * block_levels(own_key, extent, cuts, -0.22, 0.18)
    return jnp.clip(array, -bound, bound).astype(dtype)


def setup_inputs(seed: int = 0) -> dict:
    streams_of = jax.random.split(jax.random.key(seed), 4)
    return {
        "initial": centred(streams_of[0], (NTR, NX, NY, NZ), 1.0, 6.0, ((1, 32),), jnp.float32),
        "velocity": jnp.clip(jax.random.uniform(streams_of[1], (3, NX, NY, NZ), jnp.float32, -0.5, 0.5) * block_levels(streams_of[1], (3, NX, NY, NZ), ((1, 32),), -0.4, 0.0), -0.5, 0.5),
        "diffusivity": jnp.clip(jnp.exp(math.log(0.6) - 1.7917595 * jax.random.uniform(streams_of[2], (NX, NY, NZ), jnp.float32) ** block_levels(streams_of[2], (NX, NY, NZ), ((0, 32),), -0.2, 0.2)), 0.1, 0.6),
    }


step_length = 0.25
half_step = 0.125


def stencil(padded, velocity, diffusivity):
    centre = padded[..., 1:-1, :, :]
    x_plus = padded[..., 2:, :, :]
    x_minus = padded[..., :-2, :, :]
    y_plus = jnp.roll(centre, -1, axis=-2)
    y_minus = jnp.roll(centre, 1, axis=-2)
    z_plus = jnp.roll(centre, -1, axis=-1)
    z_minus = jnp.roll(centre, 1, axis=-1)
    laplace = ((x_plus + x_minus) + (y_plus + y_minus)) + (z_plus + z_minus) - 6.0 * centre
    transport = velocity[0] * (x_plus - x_minus) + velocity[1] * (y_plus - y_minus) + velocity[2] * (z_plus - z_minus)
    return diffusivity * laplace - 0.5 * transport


def operate(field, velocity, diffusivity):
    widths = [(0, 0)] * (field.ndim - 3) + [(1, 1), (0, 0), (0, 0)]
    return stencil(jnp.pad(field, widths), velocity, diffusivity)


def reference(initial, velocity, diffusivity):
    nodes = None
    fine_end = None
    for sweep in range(SWEEPS):
        if sweep == 0:
            guess = initial
            guesses = [guess]
            for slice_index in range(NT - 1):
                guess = guess + step_length * operate(guess, velocity, diffusivity)
                guesses.append(guess)
            starts = jnp.stack(guesses, axis=0)
            old_zero = operate(starts, velocity, diffusivity)
            old_one = old_zero
            old_two = old_zero
            start_image = old_zero
        else:
            starts = jnp.concatenate([initial[None], fine_end[:-1]], axis=0)
            olds = operate(nodes, velocity, diffusivity)
            old_zero = olds[:, 0]
            old_one = olds[:, 1]
            old_two = olds[:, 2]
            start_image = operate(starts, velocity, diffusivity)
        middle = starts + half_step * (start_image - old_zero) + step_length * ((5.0 / 24.0) * old_zero + (1.0 / 3.0) * old_one - (1.0 / 24.0) * old_two)
        middle_image = operate(middle, velocity, diffusivity)
        end_new = middle + half_step * (middle_image - old_one) + step_length * (-(1.0 / 24.0) * old_zero + (1.0 / 3.0) * old_one + (5.0 / 24.0) * old_two)
        end_image = operate(end_new, velocity, diffusivity)
        forcing = step_length * ((start_image + 4.0 * middle_image + end_image) / 6.0 - start_image)
        coarse = initial
        coarse_starts = []
        coarse_ends = []
        for slice_index in range(NT):
            ending = (coarse + step_length * operate(coarse, velocity, diffusivity)) + forcing[slice_index]
            coarse_starts.append(coarse)
            coarse_ends.append(ending)
            coarse = ending
        first_nodes = jnp.stack(coarse_starts, axis=0)
        last_nodes = jnp.stack(coarse_ends, axis=0)
        middle_nodes = middle + 0.5 * ((first_nodes - starts) + (last_nodes - end_new))
        nodes = jnp.stack([first_nodes, middle_nodes, last_nodes], axis=1)
        fine_end = end_new
    return nodes
```

```python
import functools
from fractions import Fraction
from math import comb

import jax
import jax.numpy as jnp
import numpy as np
from jax import lax
from jax.experimental import pallas as pl
from jax.experimental.pallas import tpu as pltpu
from jax.sharding import PartitionSpec as P

SWEEPS = 2
SLICES = 8
DT = 0.25
SHIFT = 0.875
MESH = pl.DeviceIdType.MESH


def combine(*terms):
    total = [Fraction(0)] * max(len(p) for _, p in terms)
    for factor, p in terms:
        for k, a in enumerate(p):
            total[k] += Fraction(factor) * a
    return total


def node_polynomials():
    third, small, large = Fraction(1, 3), Fraction(1, 24), Fraction(5, 24)
    half, sixth = Fraction(1, 2), Fraction(1, 6)
    start = [Fraction(1)]

    def image(p):
        return [Fraction(0)] + list(p)

    guesses = [start]
    for _ in range(SLICES - 1):
        guesses.append(combine((1, guesses[-1]), (1, image(guesses[-1]))))
    nodes = [(g, g, g) for g in guesses]
    fine_ends = None
    for sweep in range(SWEEPS):
        starts = guesses if sweep == 0 else [start] + fine_ends[:-1]
        coarse, new_nodes, new_ends = start, [], []
        for n in range(SLICES):
            s = starts[n]
            o0, o1, o2 = (image(u) for u in nodes[n])
            g0 = image(s)
            m = combine((1, s), (half, g0), (-half, o0), (large, o0), (third, o1), (-small, o2))
            g1 = image(m)
            e = combine((1, m), (half, g1), (-half, o1), (-small, o0), (third, o1), (large, o2))
            g2 = image(e)
            c = combine((sixth, g0), (4 * sixth, g1), (sixth, g2), (-1, g0))
            z = combine((1, coarse), (1, image(coarse)), (1, c))
            middle = combine((1, m), (half, coarse), (-half, s), (half, z), (-half, e))
            new_nodes.append((coarse, middle, z))
            new_ends.append(e)
            coarse = z
        nodes, fine_ends = new_nodes, new_ends
    return nodes


def shifted_powers(p, count):
    c = Fraction(SHIFT)
    out = [Fraction(0)] * max(count, len(p))
    for k, a in enumerate(p):
        for j in range(k + 1):
            out[j] += a * comb(k, j) * (-c) ** (k - j)
    assert not any(out[count:])
    return [float(a) for a in out[:count]]


DEGREE = SLICES - 1 + 3 * SWEEPS
W1 = (DEGREE + 1) // 2
W2 = DEGREE - W1
SUMS = 5


def weights():
    nodes = node_polynomials()
    table = []
    for a in range(0, SLICES, 2):
        five = (nodes[a][0], nodes[a][1], nodes[a + 1][0], nodes[a + 1][1], nodes[a + 1][2])
        assert nodes[a][2] == nodes[a + 1][0]
        table.append([shifted_powers(p, DEGREE + 1) for p in five])
    return np.array(table, np.float32)


def kernel(planes, table, initial, velocity, diffusivity, out, power, vel, dif, stencil, sums,
           local_sem, send1, recv1, send2, recv2, send3, recv3):
    count = lax.axis_size("space")
    me = lax.axis_index("space")
    tm = lax.axis_index("tm")
    core = lax.rem(tm, 2)
    pair = lax.div(tm, 2)
    peer = tm + 1 - 2 * core
    has_left = me > 0
    has_right = me < count - 1
    first = 2 * core
    own = pl.ds(W1, planes)

    barrier = pltpu.get_barrier_semaphore()

    @pl.when(has_left)
    def _():
        pl.semaphore_signal(barrier, inc=1, device_id={"space": me - 1}, device_id_type=MESH)

    @pl.when(has_right)
    def _():
        pl.semaphore_signal(barrier, inc=1, device_id={"space": me + 1}, device_id_type=MESH)

    pl.semaphore_signal(barrier, inc=1, device_id={"tm": peer}, device_id_type=MESH)

    loads = [
        pltpu.make_async_copy(initial.at[pl.ds(first, 2)], power.at[0, :, own], local_sem.at[0]),
        pltpu.make_async_copy(velocity, vel.at[:, pl.ds(W1 - 1, planes)], local_sem.at[1]),
        pltpu.make_async_copy(diffusivity, dif.at[pl.ds(W1 - 1, planes)], local_sem.at[2]),
    ]
    for copy in loads:
        copy.start()

    pl.semaphore_wait(barrier, 1 + has_left.astype(jnp.int32) + has_right.astype(jnp.int32))

    def remote(src, dst, send, recv, to):
        return pltpu.make_async_remote_copy(
            src_ref=src, dst_ref=dst, send_sem=send, recv_sem=recv, device_id={"space": to}, device_id_type=MESH
        )

    halo = W1 - 1
    low, high = pl.ds(0, W1), pl.ds(W1 + planes, W1)
    low_c, high_c = pl.ds(0, halo), pl.ds(halo + planes, halo)
    top, bottom = pl.ds(planes - W1, W1), pl.ds(0, W1)
    top_c, bottom_c = pl.ds(planes - halo, halo), pl.ds(0, halo)
    two = pl.ds(first, 2)
    right = jnp.minimum(me + 1, count - 1)
    left = jnp.maximum(me - 1, 0)
    to_right = [
        remote(initial.at[two, top], power.at[0, :, low], send1.at[0, 0], recv1.at[0, 0], right),
        remote(velocity.at[:, top_c], vel.at[:, low_c], send1.at[0, 1], recv1.at[0, 1], right),
        remote(diffusivity.at[top_c], dif.at[low_c], send1.at[0, 2], recv1.at[0, 2], right),
    ]
    to_left = [
        remote(initial.at[two, bottom], power.at[0, :, high], send1.at[1, 0], recv1.at[1, 0], left),
        remote(velocity.at[:, bottom_c], vel.at[:, high_c], send1.at[1, 1], recv1.at[1, 1], left),
        remote(diffusivity.at[bottom_c], dif.at[high_c], send1.at[1, 2], recv1.at[1, 2], left),
    ]

    @pl.when(has_right)
    def _():
        for copy in to_right:
            copy.start()

    @pl.when(has_left)
    def _():
        for copy in to_left:
            copy.start()

    low2, high2 = pl.ds(W1 - W2, W2), pl.ds(W1 + planes, W2)

    @pl.when(jnp.logical_not(has_left))
    def _():
        power[0, :, low] = jnp.zeros((2, W1) + power.shape[3:], jnp.float32)
        power[W1, :, low2] = jnp.zeros((2, W2) + power.shape[3:], jnp.float32)
        vel[:, low_c] = jnp.zeros((3, halo) + power.shape[3:], jnp.float32)
        dif[low_c] = jnp.zeros((halo,) + power.shape[3:], jnp.float32)

    @pl.when(jnp.logical_not(has_right))
    def _():
        power[0, :, high] = jnp.zeros((2, W1) + power.shape[3:], jnp.float32)
        power[W1, :, high2] = jnp.zeros((2, W2) + power.shape[3:], jnp.float32)
        vel[:, high_c] = jnp.zeros((3, halo) + power.shape[3:], jnp.float32)
        dif[high_c] = jnp.zeros((halo,) + power.shape[3:], jnp.float32)

    def derive(lo, hi):
        def one(q, carry):
            d = DT * dif[q]
            for axis in range(3):
                v = (0.5 * DT) * vel[axis, q]
                stencil[2 * axis, q] = d - v
                stencil[2 * axis + 1, q] = d + v
            stencil[6, q] = SHIFT - 6.0 * d
            return carry

        lax.fori_loop(lo, hi, one, 0, unroll=2)

    def advance(k, lo, hi):
        def one(q, carry):
            c = [stencil[j, q - 1] for j in range(7)]
            for t in range(2):
                u = power[k - 1, t, q]
                x = c[0] * power[k - 1, t, q + 1] + c[1] * power[k - 1, t, q - 1]
                y = c[2] * pltpu.roll(u, u.shape[0] - 1, 0) + c[3] * pltpu.roll(u, 1, 0)
                z = c[4] * pltpu.roll(u, u.shape[1] - 1, 1) + c[5] * pltpu.roll(u, 1, 1)
                power[k, t, q] = (x + y) + (z + c[6] * u)
            return carry

        lax.fori_loop(lo, hi, one, 0, unroll=2)

    for copy in loads:
        copy.wait()
    derive(halo, halo + planes)

    @pl.when(has_right)
    def _():
        for copy in to_right:
            copy.wait_send()
        for copy in to_left:
            copy.wait_recv()

    @pl.when(has_left)
    def _():
        for copy in to_left:
            copy.wait_send()
        for copy in to_right:
            copy.wait_recv()

    derive(0, halo)
    derive(halo + planes, 2 * halo + planes)
    for k in range(1, W1 + 1):
        advance(k, k, 2 * W1 + planes - k)

    again_right = remote(
        power.at[W1, :, pl.ds(W1 + planes - W2, W2)], power.at[W1, :, low2], send2.at[0], recv2.at[0], right
    )
    again_left = remote(power.at[W1, :, pl.ds(W1, W2)], power.at[W1, :, high2], send2.at[1], recv2.at[1], left)

    @pl.when(has_right)
    def _():
        again_right.start()

    @pl.when(has_left)
    def _():
        again_left.start()

    def accumulate(lo, hi):
        def one(q, carry):
            for t in range(2):
                v = [power[k, t, q + W1] for k in range(lo, hi)]
                for j in range(SUMS):
                    total = sums[j, t, q] if lo else None
                    for k in range(lo, hi):
                        term = table[(pair * SUMS + j) * (DEGREE + 1) + k] * v[k - lo]
                        total = term if total is None else total + term
                    sums[j, t, q] = total
            return carry

        lax.fori_loop(0, planes, one, 0)

    accumulate(0, W1 + 1)

    @pl.when(has_right)
    def _():
        again_right.wait_send()
        again_left.wait_recv()

    @pl.when(has_left)
    def _():
        again_left.wait_send()
        again_right.wait_recv()

    for k in range(W1 + 1, DEGREE + 1):
        advance(k, 1 + k - W1, 2 * W1 + planes - 1 - (k - W1))
    accumulate(W1 + 1, DEGREE + 1)

    across = pltpu.make_async_remote_copy(
        src_ref=sums.at[pl.ds(2 - 2 * core, 3)],
        dst_ref=out.at[:, two],
        send_sem=send3,
        recv_sem=recv3,
        device_id={"tm": peer},
        device_id_type=MESH,
    )
    across.start()
    keep = pltpu.make_async_copy(sums.at[pl.ds(2 * core, 3)], out.at[:, two], local_sem.at[3])
    keep.start()
    keep.wait()
    across.wait()


def body(initial, velocity, diffusivity):
    planes, rows, lanes = diffusivity.shape
    table = jnp.asarray(weights().reshape(-1))
    anywhere = pl.BlockSpec(memory_space=pl.ANY)
    halo = W1 - 1
    nodes = pl.pallas_call(
        functools.partial(kernel, planes),
        out_shape=jax.ShapeDtypeStruct((3,) + initial.shape, jnp.float32),
        in_specs=[pl.BlockSpec(memory_space=pltpu.SMEM), anywhere, anywhere, anywhere],
        out_specs=anywhere,
        scratch_shapes=[
            pltpu.VMEM((DEGREE + 1, 2, planes + 2 * W1, rows, lanes), jnp.float32),
            pltpu.VMEM((3, planes + 2 * halo, rows, lanes), jnp.float32),
            pltpu.VMEM((planes + 2 * halo, rows, lanes), jnp.float32),
            pltpu.VMEM((7, planes + 2 * halo, rows, lanes), jnp.float32),
            pltpu.VMEM((SUMS, 2, planes, rows, lanes), jnp.float32),
            pltpu.SemaphoreType.DMA((4,)),
            pltpu.SemaphoreType.DMA((2, 3)),
            pltpu.SemaphoreType.DMA((2, 3)),
            pltpu.SemaphoreType.DMA((2,)),
            pltpu.SemaphoreType.DMA((2,)),
            pltpu.SemaphoreType.DMA,
            pltpu.SemaphoreType.DMA,
        ],
        compiler_params=pltpu.CompilerParams(collective_id=0, has_side_effects=True, vmem_limit_bytes=24 * 2**20),
        name="powers",
    )(table, initial, velocity, diffusivity)
    return nodes[None]


def solution(mesh):
    return jax.shard_map(
        body,
        mesh=mesh,
        in_specs=(
            P(None, "space", None, None),
            P(None, "space", None, None),
            P("space", None, None),
        ),
        out_specs=P("tm", None, None, "space", None, None),
        check_vma=False,
    )
```

```python
import functools
from fractions import Fraction
from math import comb

import jax
import jax.numpy as jnp
import numpy as np
from jax import lax
from jax.experimental import pallas as pl
from jax.experimental.pallas import tpu as pltpu
from jax.sharding import PartitionSpec as P

SWEEPS = 2
SLICES = 8
DT = 0.25
SHIFT = 0.875
MESH = pl.DeviceIdType.MESH


def combine(*terms):
    total = [Fraction(0)] * max(len(p) for _, p in terms)
    for factor, p in terms:
        for k, a in enumerate(p):
            total[k] += Fraction(factor) * a
    return total


def node_polynomials():
    third, small, large = Fraction(1, 3), Fraction(1, 24), Fraction(5, 24)
    half, sixth = Fraction(1, 2), Fraction(1, 6)
    start = [Fraction(1)]

    def image(p):
        return [Fraction(0)] + list(p)

    guesses = [start]
    for _ in range(SLICES - 1):
        guesses.append(combine((1, guesses[-1]), (1, image(guesses[-1]))))
    nodes = [(g, g, g) for g in guesses]
    fine_ends = None
    for sweep in range(SWEEPS):
        starts = guesses if sweep == 0 else [start] + fine_ends[:-1]
        coarse, new_nodes, new_ends = start, [], []
        for n in range(SLICES):
            s = starts[n]
            o0, o1, o2 = (image(u) for u in nodes[n])
            g0 = image(s)
            m = combine((1, s), (half, g0), (-half, o0), (large, o0), (third, o1), (-small, o2))
            g1 = image(m)
            e = combine((1, m), (half, g1), (-half, o1), (-small, o0), (third, o1), (large, o2))
            g2 = image(e)
            c = combine((sixth, g0), (4 * sixth, g1), (sixth, g2), (-1, g0))
            z = combine((1, coarse), (1, image(coarse)), (1, c))
            middle = combine((1, m), (half, coarse), (-half, s), (half, z), (-half, e))
            new_nodes.append((coarse, middle, z))
            new_ends.append(e)
            coarse = z
        nodes, fine_ends = new_nodes, new_ends
    return nodes


def shifted_powers(p, count):
    c = Fraction(SHIFT)
    out = [Fraction(0)] * max(count, len(p))
    for k, a in enumerate(p):
        for j in range(k + 1):
            out[j] += a * comb(k, j) * (-c) ** (k - j)
    assert not any(out[count:])
    return [float(a) for a in out[:count]]


DEGREE = SLICES - 1 + 3 * SWEEPS
W1 = (DEGREE + 1) // 2
W2 = DEGREE - W1
SUMS = 5


def weights():
    nodes = node_polynomials()
    table = []
    for a in range(0, SLICES, 2):
        five = (nodes[a][0], nodes[a][1], nodes[a + 1][0], nodes[a + 1][1], nodes[a + 1][2])
        assert nodes[a][2] == nodes[a + 1][0]
        table.append([shifted_powers(p, DEGREE + 1) for p in five])
    return np.array(table, np.float32)


def kernel(planes, table, initial, velocity, diffusivity, out, power, vel, dif, stencil, sums,
           local_sem, send1, recv1, send2, recv2, send3, recv3):
    count = lax.axis_size("space")
    me = lax.axis_index("space")
    tm = lax.axis_index("tm")
    core = lax.rem(tm, 2)
    pair = lax.div(tm, 2)
    peer = tm + 1 - 2 * core
    has_left = me > 0
    has_right = me < count - 1
    first = 2 * core
    own = pl.ds(W1, planes)

    barrier = pltpu.get_barrier_semaphore()

    @pl.when(has_left)
    def _():
        pl.semaphore_signal(barrier, inc=1, device_id={"space": me - 1}, device_id_type=MESH)

    @pl.when(has_right)
    def _():
        pl.semaphore_signal(barrier, inc=1, device_id={"space": me + 1}, device_id_type=MESH)

    pl.semaphore_signal(barrier, inc=1, device_id={"tm": peer}, device_id_type=MESH)

    loads = [
        pltpu.make_async_copy(initial.at[pl.ds(first, 2)], power.at[0, :, own], local_sem.at[0]),
        pltpu.make_async_copy(velocity, vel.at[:, pl.ds(W1 - 1, planes)], local_sem.at[1]),
        pltpu.make_async_copy(diffusivity, dif.at[pl.ds(W1 - 1, planes)], local_sem.at[2]),
    ]
    for copy in loads:
        copy.start()

    pl.semaphore_wait(barrier, 1 + has_left.astype(jnp.int32) + has_right.astype(jnp.int32))

    def remote(src, dst, send, recv, to):
        return pltpu.make_async_remote_copy(
            src_ref=src, dst_ref=dst, send_sem=send, recv_sem=recv, device_id={"space": to}, device_id_type=MESH
        )

    halo = W1 - 1
    low, high = pl.ds(0, W1), pl.ds(W1 + planes, W1)
    low_c, high_c = pl.ds(0, halo), pl.ds(halo + planes, halo)
    top, bottom = pl.ds(planes - W1, W1), pl.ds(0, W1)
    top_c, bottom_c = pl.ds(planes - halo, halo), pl.ds(0, halo)
    two = pl.ds(first, 2)
    right = jnp.minimum(me + 1, count - 1)
    left = jnp.maximum(me - 1, 0)
    to_right = [
        remote(initial.at[two, top], power.at[0, :, low], send1.at[0, 0], recv1.at[0, 0], right),
        remote(velocity.at[:, top_c], vel.at[:, low_c], send1.at[0, 1], recv1.at[0, 1], right),
        remote(diffusivity.at[top_c], dif.at[low_c], send1.at[0, 2], recv1.at[0, 2], right),
    ]
    to_left = [
        remote(initial.at[two, bottom], power.at[0, :, high], send1.at[1, 0], recv1.at[1, 0], left),
        remote(velocity.at[:, bottom_c], vel.at[:, high_c], send1.at[1, 1], recv1.at[1, 1], left),
        remote(diffusivity.at[bottom_c], dif.at[high_c], send1.at[1, 2], recv1.at[1, 2], left),
    ]

    @pl.when(has_right)
    def _():
        for copy in to_right:
            copy.start()

    @pl.when(has_left)
    def _():
        for copy in to_left:
            copy.start()

    low2, high2 = pl.ds(W1 - W2, W2), pl.ds(W1 + planes, W2)

    @pl.when(jnp.logical_not(has_left))
    def _():
        power[0, :, low] = jnp.zeros((2, W1) + power.shape[3:], jnp.float32)
        power[W1, :, low2] = jnp.zeros((2, W2) + power.shape[3:], jnp.float32)
        vel[:, low_c] = jnp.zeros((3, halo) + power.shape[3:], jnp.float32)
        dif[low_c] = jnp.zeros((halo,) + power.shape[3:], jnp.float32)

    @pl.when(jnp.logical_not(has_right))
    def _():
        power[0, :, high] = jnp.zeros((2, W1) + power.shape[3:], jnp.float32)
        power[W1, :, high2] = jnp.zeros((2, W2) + power.shape[3:], jnp.float32)
        vel[:, high_c] = jnp.zeros((3, halo) + power.shape[3:], jnp.float32)
        dif[high_c] = jnp.zeros((halo,) + power.shape[3:], jnp.float32)

    def derive(lo, hi):
        def one(q, carry):
            d = DT * dif[q]
            for axis in range(3):
                v = (0.5 * DT) * vel[axis, q]
                stencil[2 * axis, q] = d - v
                stencil[2 * axis + 1, q] = d + v
            stencil[6, q] = SHIFT - 6.0 * d
            return carry

        lax.fori_loop(lo, hi, one, 0, unroll=2)

    def advance(k, lo, hi):
        def one(q, carry):
            c = [stencil[j, q - 1] for j in range(7)]
            for t in range(2):
                u = power[k - 1, t, q]
                x = c[0] * power[k - 1, t, q + 1] + c[1] * power[k - 1, t, q - 1]
                y = c[2] * pltpu.roll(u, u.shape[0] - 1, 0) + c[3] * pltpu.roll(u, 1, 0)
                z = c[4] * pltpu.roll(u, u.shape[1] - 1, 1) + c[5] * pltpu.roll(u, 1, 1)
                power[k, t, q] = (x + y) + (z + c[6] * u)
            return carry

        lax.fori_loop(lo, hi, one, 0, unroll=True)

    for copy in loads:
        copy.wait()
    derive(halo, halo + planes)

    @pl.when(has_right)
    def _():
        for copy in to_right:
            copy.wait_send()
        for copy in to_left:
            copy.wait_recv()

    @pl.when(has_left)
    def _():
        for copy in to_left:
            copy.wait_send()
        for copy in to_right:
            copy.wait_recv()

    derive(0, halo)
    derive(halo + planes, 2 * halo + planes)
    for k in range(1, W1 + 1):
        advance(k, k, 2 * W1 + planes - k)

    again_right = remote(
        power.at[W1, :, pl.ds(W1 + planes - W2, W2)], power.at[W1, :, low2], send2.at[0], recv2.at[0], right
    )
    again_left = remote(power.at[W1, :, pl.ds(W1, W2)], power.at[W1, :, high2], send2.at[1], recv2.at[1], left)

    @pl.when(has_right)
    def _():
        again_right.start()

    @pl.when(has_left)
    def _():
        again_left.start()

    def accumulate(lo, hi):
        def one(q, carry):
            for t in range(2):
                v = [power[k, t, q + W1] for k in range(lo, hi)]
                for j in range(SUMS):
                    total = sums[j, t, q] if lo else None
                    for k in range(lo, hi):
                        term = table[(pair * SUMS + j) * (DEGREE + 1) + k] * v[k - lo]
                        total = term if total is None else total + term
                    sums[j, t, q] = total
            return carry

        lax.fori_loop(0, planes, one, 0)

    accumulate(0, W1 + 1)

    @pl.when(has_right)
    def _():
        again_right.wait_send()
        again_left.wait_recv()

    @pl.when(has_left)
    def _():
        again_left.wait_send()
        again_right.wait_recv()

    for k in range(W1 + 1, DEGREE + 1):
        advance(k, 1 + k - W1, 2 * W1 + planes - 1 - (k - W1))
    accumulate(W1 + 1, DEGREE + 1)

    across = pltpu.make_async_remote_copy(
        src_ref=sums.at[pl.ds(2 - 2 * core, 3)],
        dst_ref=out.at[:, two],
        send_sem=send3,
        recv_sem=recv3,
        device_id={"tm": peer},
        device_id_type=MESH,
    )
    across.start()
    keep = pltpu.make_async_copy(sums.at[pl.ds(2 * core, 3)], out.at[:, two], local_sem.at[3])
    keep.start()
    keep.wait()
    across.wait()


def body(initial, velocity, diffusivity):
    planes, rows, lanes = diffusivity.shape
    table = jnp.asarray(weights().reshape(-1))
    anywhere = pl.BlockSpec(memory_space=pl.ANY)
    halo = W1 - 1
    nodes = pl.pallas_call(
        functools.partial(kernel, planes),
        out_shape=jax.ShapeDtypeStruct((3,) + initial.shape, jnp.float32),
        in_specs=[pl.BlockSpec(memory_space=pltpu.SMEM), anywhere, anywhere, anywhere],
        out_specs=anywhere,
        scratch_shapes=[
            pltpu.VMEM((DEGREE + 1, 2, planes + 2 * W1, rows, lanes), jnp.float32),
            pltpu.VMEM((3, planes + 2 * halo, rows, lanes), jnp.float32),
            pltpu.VMEM((planes + 2 * halo, rows, lanes), jnp.float32),
            pltpu.VMEM((7, planes + 2 * halo, rows, lanes), jnp.float32),
            pltpu.VMEM((SUMS, 2, planes, rows, lanes), jnp.float32),
            pltpu.SemaphoreType.DMA((4,)),
            pltpu.SemaphoreType.DMA((2, 3)),
            pltpu.SemaphoreType.DMA((2, 3)),
            pltpu.SemaphoreType.DMA((2,)),
            pltpu.SemaphoreType.DMA((2,)),
            pltpu.SemaphoreType.DMA,
            pltpu.SemaphoreType.DMA,
        ],
        compiler_params=pltpu.CompilerParams(collective_id=0, has_side_effects=True, vmem_limit_bytes=24 * 2**20),
        name="powers",
    )(table, *[pltpu.with_memory_space_constraint(a, pltpu.HBM) for a in (initial, velocity, diffusivity)])
    return nodes[None]


def solution(mesh):
    return jax.shard_map(
        body,
        mesh=mesh,
        in_specs=(
            P(None, "space", None, None),
            P(None, "space", None, None),
            P("space", None, None),
        ),
        out_specs=P("tm", None, None, "space", None, None),
        check_vma=False,
    )
```

```python
import functools
from fractions import Fraction
from math import comb

import jax
import jax.numpy as jnp
import numpy as np
from jax import lax
from jax.experimental import pallas as pl
from jax.experimental.pallas import tpu as pltpu
from jax.sharding import PartitionSpec as P

SWEEPS = 2
SLICES = 8
DT = 0.25
SHIFT = 0.875
MESH = pl.DeviceIdType.MESH


def combine(*terms):
    total = [Fraction(0)] * max(len(p) for _, p in terms)
    for factor, p in terms:
        for k, a in enumerate(p):
            total[k] += Fraction(factor) * a
    return total


def node_polynomials():
    third, small, large = Fraction(1, 3), Fraction(1, 24), Fraction(5, 24)
    half, sixth = Fraction(1, 2), Fraction(1, 6)
    start = [Fraction(1)]

    def image(p):
        return [Fraction(0)] + list(p)

    guesses = [start]
    for _ in range(SLICES - 1):
        guesses.append(combine((1, guesses[-1]), (1, image(guesses[-1]))))
    nodes = [(g, g, g) for g in guesses]
    fine_ends = None
    for sweep in range(SWEEPS):
        starts = guesses if sweep == 0 else [start] + fine_ends[:-1]
        coarse, new_nodes, new_ends = start, [], []
        for n in range(SLICES):
            s = starts[n]
            o0, o1, o2 = (image(u) for u in nodes[n])
            g0 = image(s)
            m = combine((1, s), (half, g0), (-half, o0), (large, o0), (third, o1), (-small, o2))
            g1 = image(m)
            e = combine((1, m), (half, g1), (-half, o1), (-small, o0), (third, o1), (large, o2))
            g2 = image(e)
            c = combine((sixth, g0), (4 * sixth, g1), (sixth, g2), (-1, g0))
            z = combine((1, coarse), (1, image(coarse)), (1, c))
            middle = combine((1, m), (half, coarse), (-half, s), (half, z), (-half, e))
            new_nodes.append((coarse, middle, z))
            new_ends.append(e)
            coarse = z
        nodes, fine_ends = new_nodes, new_ends
    return nodes


def shifted_powers(p, count):
    c = Fraction(SHIFT)
    out = [Fraction(0)] * max(count, len(p))
    for k, a in enumerate(p):
        for j in range(k + 1):
            out[j] += a * comb(k, j) * (-c) ** (k - j)
    assert not any(out[count:])
    return [float(a) for a in out[:count]]


DEGREE = SLICES - 1 + 3 * SWEEPS
W1 = 5
W2 = DEGREE - W1
EDGE = max(W1, W2)
HALO = EDGE - 1
NEAR = W1 - 1
FAR = HALO - NEAR
SUMS = 5
LANES = 128


def weights():
    nodes = node_polynomials()
    table = np.zeros((SLICES, LANES), np.float32)
    for n in range(SLICES):
        a = n - n % 2
        assert nodes[a][2] == nodes[a + 1][0]
        own, other = (nodes[a][:2], nodes[a + 1][1:]) if n == a else (nodes[a + 1][1:], nodes[a][:2])
        row = [shifted_powers(p, DEGREE + 1) for p in (nodes[a][2], *own, *other)]
        table[n, : SUMS * (DEGREE + 1)] = np.reshape(row, -1)
    return table


def kernel(planes, weight_rows, initial, velocity, diffusivity, out, power, raw, stencil, sums, across, weight,
           local_sem, send, recv, pass_send, pass_recv, cross_send, cross_recv):
    count = lax.axis_size("space")
    me = lax.axis_index("space")
    tm = lax.axis_index("tm")
    core = lax.rem(tm, 2)
    peer = tm + 1 - 2 * core
    has_left = me > 0
    has_right = me < count - 1
    left = jnp.maximum(me - 1, 0)
    right = jnp.minimum(me + 1, count - 1)
    first = 2 * core
    two = pl.ds(first, 2)
    tile = power.shape[3:]

    barrier = pltpu.get_barrier_semaphore()

    @pl.when(has_left)
    def _():
        pl.semaphore_signal(barrier, inc=1, device_id={"space": me - 1}, device_id_type=MESH)

    @pl.when(has_right)
    def _():
        pl.semaphore_signal(barrier, inc=1, device_id={"space": me + 1}, device_id_type=MESH)

    pl.semaphore_signal(barrier, inc=1, device_id={"tm": peer}, device_id_type=MESH)

    loads = [
        pltpu.make_async_copy(velocity, raw.at[pl.ds(0, 3), pl.ds(HALO, planes)], local_sem.at[0]),
        pltpu.make_async_copy(diffusivity, raw.at[3, pl.ds(HALO, planes)], local_sem.at[1]),
        pltpu.make_async_copy(initial.at[two], power.at[0, :, pl.ds(EDGE, planes)], local_sem.at[2]),
        pltpu.make_async_copy(weight_rows, weight, local_sem.at[3]),
    ]
    for copy in loads:
        copy.start()

    def clear(edge, halo):
        power[0, :, pl.ds(edge, EDGE)] = jnp.zeros((2, EDGE) + tile, jnp.float32)
        power[W1, :, pl.ds(edge, EDGE)] = jnp.zeros((2, EDGE) + tile, jnp.float32)
        raw[:, pl.ds(halo, HALO)] = jnp.zeros((4, HALO) + tile, jnp.float32)

    @pl.when(jnp.logical_not(has_left))
    def _():
        clear(0, 0)

    @pl.when(jnp.logical_not(has_right))
    def _():
        clear(EDGE + planes, HALO + planes)

    def remote(side, item, src, dst):
        return pltpu.make_async_remote_copy(
            src_ref=src,
            dst_ref=dst,
            send_sem=send.at[side, item],
            recv_sem=recv.at[side, item],
            device_id={"space": left if side else right},
            device_id_type=MESH,
        )

    def field_halo(side, item, level, t, width):
        src = EDGE if side else EDGE + planes - width
        dst = EDGE + planes if side else EDGE - width
        return remote(side, item, power.at[level, t, pl.ds(src, width)], power.at[level, t, pl.ds(dst, width)])

    def near_at(side):
        return pl.ds(HALO + planes if side else HALO - NEAR, NEAR)

    def far_at(side):
        return pl.ds(HALO + planes + NEAR if side else 0, FAR)

    def passed(item, side, at):
        ref = raw.at[two, at]
        return pltpu.make_async_remote_copy(
            src_ref=ref,
            dst_ref=ref,
            send_sem=pass_send.at[item, side],
            recv_sem=pass_recv.at[item, side],
            device_id={"tm": peer},
            device_id_type=MESH,
        )

    near, far, first_round, second_round, near_pass, far_pass = [], [], [[], []], [[], []], [], []
    for side in range(2):
        src = HALO if side else HALO + planes - NEAR
        near.append(remote(side, 0, raw.at[two, pl.ds(src, NEAR)], raw.at[two, near_at(side)]))
        src = HALO + NEAR if side else HALO + planes - HALO
        far.append(remote(side, 1, raw.at[two, pl.ds(src, FAR)], raw.at[two, far_at(side)]))
        near_pass.append(passed(0, side, near_at(side)))
        far_pass.append(passed(1, side, far_at(side)))
        for t in range(2):
            first_round[t].append(field_halo(side, 2 + t, 0, t, W1))
            second_round[t].append(field_halo(side, 4 + t, W1, t, W2))

    def start(*pairs):
        @pl.when(has_right)
        def _():
            for pair in pairs:
                pair[0].start()

        @pl.when(has_left)
        def _():
            for pair in pairs:
                pair[1].start()

    def arrived(pair, then=None):
        @pl.when(has_left)
        def _():
            pair[0].wait_recv()
            if then:
                then[0].start()

        @pl.when(has_right)
        def _():
            pair[1].wait_recv()
            if then:
                then[1].start()

    def derive(lo, hi):
        for q in range(lo, hi):
            d = DT * raw[3, q]
            for axis in range(3):
                v = (0.5 * DT) * raw[axis, q]
                stencil[2 * axis, q] = d - v
                stencil[2 * axis + 1, q] = d + v
            stencil[6, q] = SHIFT - 6.0 * d

    def advance(t, k, lo, hi):
        for q in range(lo, hi):
            c = [stencil[j, q - 1] for j in range(7)]
            u = power[k - 1, t, q]
            x = c[0] * power[k - 1, t, q + 1] + c[1] * power[k - 1, t, q - 1]
            y = c[2] * pltpu.roll(u, u.shape[0] - 1, 0) + c[3] * pltpu.roll(u, 1, 0)
            z = c[4] * pltpu.roll(u, u.shape[1] - 1, 1) + c[5] * pltpu.roll(u, 1, 1)
            power[k, t, q] = (x + y) + (z + c[6] * u)

    def accumulate(t, p, lo, hi, before):
        v = [power[k, t, p + EDGE] for k in range(lo, hi)]
        totals = []
        for j in range(SUMS):
            total = before[j] if before else None
            for k in range(lo, hi):
                term = weight[tm, j * (DEGREE + 1) + k] * v[k - lo]
                total = term if total is None else total + term
            totals.append(total)
        return totals

    for copy in loads:
        copy.wait()
    derive(HALO, HALO + planes)

    pl.semaphore_wait(barrier, 1 + has_left.astype(jnp.int32) + has_right.astype(jnp.int32))
    start(near, first_round[0], first_round[1], far)

    arrived(near, near_pass)
    arrived(near_pass)
    derive(HALO - NEAR, HALO)
    derive(HALO + planes, HALO + planes + NEAR)
    for t in range(2):
        arrived(first_round[t])
        for k in range(1, W1 + 1):
            advance(t, k, EDGE - W1 + k, EDGE + planes + W1 - k)
        start(second_round[t])

    arrived(far, far_pass)
    for t in range(2):
        for p in range(planes):
            for j, total in enumerate(accumulate(t, p, 0, W1 + 1, None)):
                sums[j, t, p] = total
    arrived(far_pass)
    derive(0, FAR)
    derive(HALO + planes + NEAR, 2 * HALO + planes)

    crossings = []
    for t in range(2):
        arrived(second_round[t])
        for j in range(1, W2 + 1):
            advance(t, W1 + j, EDGE - W2 + j, EDGE + planes + W2 - j)
        for p in range(planes):
            totals = accumulate(t, p, W1 + 1, DEGREE + 1, [sums[j, t, p] for j in range(SUMS)])
            out[2 - 2 * core, first + t, p] = totals[0]
            out[core, first + t, p] = totals[1]
            out[core + 1, first + t, p] = totals[2]
            across[t, 2 * core, p] = totals[0]
            across[t, 1 - core, p] = totals[3]
            across[t, 2 - core, p] = totals[4]
        crossings.append(
            pltpu.make_async_remote_copy(
                src_ref=across.at[t],
                dst_ref=out.at[:, first + t],
                send_sem=cross_send.at[t],
                recv_sem=cross_recv.at[t],
                device_id={"tm": peer},
                device_id_type=MESH,
            )
        )
        crossings[t].start()

    everything = [near, far, *first_round, *second_round]

    @pl.when(has_right)
    def _():
        for pair in everything:
            pair[0].wait_send()
        near_pass[1].wait_send()
        far_pass[1].wait_send()

    @pl.when(has_left)
    def _():
        for pair in everything:
            pair[1].wait_send()
        near_pass[0].wait_send()
        far_pass[0].wait_send()

    for copy in crossings:
        copy.wait()


def body(initial, velocity, diffusivity):
    planes, rows, lanes = diffusivity.shape
    operands = (jnp.asarray(weights()), initial, velocity, diffusivity)
    nodes = pl.pallas_call(
        functools.partial(kernel, planes),
        out_shape=jax.ShapeDtypeStruct((3,) + initial.shape, jnp.float32),
        in_specs=[pl.BlockSpec(memory_space=pl.ANY)] * 4,
        out_specs=pl.BlockSpec(memory_space=pltpu.VMEM),
        scratch_shapes=[
            pltpu.VMEM((DEGREE + 1, 2, planes + 2 * EDGE, rows, lanes), jnp.float32),
            pltpu.VMEM((4, planes + 2 * HALO, rows, lanes), jnp.float32),
            pltpu.VMEM((7, planes + 2 * HALO, rows, lanes), jnp.float32),
            pltpu.VMEM((SUMS, 2, planes, rows, lanes), jnp.float32),
            pltpu.VMEM((2, 3, planes, rows, lanes), jnp.float32),
            pltpu.SMEM((SLICES, LANES), jnp.float32),
            pltpu.SemaphoreType.DMA((4,)),
            pltpu.SemaphoreType.DMA((2, 6)),
            pltpu.SemaphoreType.DMA((2, 6)),
            pltpu.SemaphoreType.DMA((2, 2)),
            pltpu.SemaphoreType.DMA((2, 2)),
            pltpu.SemaphoreType.DMA((2,)),
            pltpu.SemaphoreType.DMA((2,)),
        ],
        compiler_params=pltpu.CompilerParams(collective_id=0, has_side_effects=True, vmem_limit_bytes=24 * 2**20),
        name="powers",
    )(*[pltpu.with_memory_space_constraint(a, pltpu.HBM) for a in operands])
    return nodes[None]


def solution(mesh):
    return jax.shard_map(
        body,
        mesh=mesh,
        in_specs=(
            P(None, "space", None, None),
            P(None, "space", None, None),
            P("space", None, None),
        ),
        out_specs=P("tm", None, None, "space", None, None),
        check_vma=False,
    )
```

```python
import functools
from fractions import Fraction
from math import comb

import jax
import jax.numpy as jnp
import numpy as np
from jax import lax
from jax.experimental import pallas as pl
from jax.experimental.pallas import tpu as pltpu
from jax.sharding import PartitionSpec as P

SWEEPS = 2
SLICES = 8
DT = 0.25
SHIFT = 0.875
MESH = pl.DeviceIdType.MESH


def combine(*terms):
    total = [Fraction(0)] * max(len(p) for _, p in terms)
    for factor, p in terms:
        for k, a in enumerate(p):
            total[k] += Fraction(factor) * a
    return total


def node_polynomials():
    third, small, large = Fraction(1, 3), Fraction(1, 24), Fraction(5, 24)
    half, sixth = Fraction(1, 2), Fraction(1, 6)
    start = [Fraction(1)]

    def image(p):
        return [Fraction(0)] + list(p)

    guesses = [start]
    for _ in range(SLICES - 1):
        guesses.append(combine((1, guesses[-1]), (1, image(guesses[-1]))))
    nodes = [(g, g, g) for g in guesses]
    fine_ends = None
    for sweep in range(SWEEPS):
        starts = guesses if sweep == 0 else [start] + fine_ends[:-1]
        coarse, new_nodes, new_ends = start, [], []
        for n in range(SLICES):
            s = starts[n]
            o0, o1, o2 = (image(u) for u in nodes[n])
            g0 = image(s)
            m = combine((1, s), (half, g0), (-half, o0), (large, o0), (third, o1), (-small, o2))
            g1 = image(m)
            e = combine((1, m), (half, g1), (-half, o1), (-small, o0), (third, o1), (large, o2))
            g2 = image(e)
            c = combine((sixth, g0), (4 * sixth, g1), (sixth, g2), (-1, g0))
            z = combine((1, coarse), (1, image(coarse)), (1, c))
            middle = combine((1, m), (half, coarse), (-half, s), (half, z), (-half, e))
            new_nodes.append((coarse, middle, z))
            new_ends.append(e)
            coarse = z
        nodes, fine_ends = new_nodes, new_ends
    return nodes


def shifted_powers(p, count):
    c = Fraction(SHIFT)
    out = [Fraction(0)] * max(count, len(p))
    for k, a in enumerate(p):
        for j in range(k + 1):
            out[j] += a * comb(k, j) * (-c) ** (k - j)
    assert not any(out[count:])
    return [float(a) for a in out[:count]]


DEGREE = SLICES - 1 + 3 * SWEEPS
W1 = 7
W2 = DEGREE - W1
EDGE = W1 + W2
HALO = EDGE - 1
NEAR = W1 - 1
SUMS = 5
GROUP = 16
LANES = 128


def weights():
    nodes = node_polynomials()
    table = np.zeros((SLICES, LANES), np.float32)
    for n in range(SLICES):
        a = n - n % 2
        assert nodes[a][2] == nodes[a + 1][0]
        own, other = (nodes[a][:2], nodes[a + 1][1:]) if n == a else (nodes[a + 1][1:], nodes[a][:2])
        row = [shifted_powers(p, DEGREE + 1) for p in (nodes[a][2], *own, *other)]
        table[n, : SUMS * (DEGREE + 1)] = np.reshape(row, -1)
    return table


def kernel(planes, weight_rows, initial, velocity, diffusivity, out, power, raw, stencil, sums, across, weight,
           local_sem, send, recv, pass_send, pass_recv, cross_send, cross_recv):
    count = lax.axis_size("space")
    me = lax.axis_index("space")
    tm = lax.axis_index("tm")
    core = lax.rem(tm, 2)
    peer = tm + 1 - 2 * core
    has_left = me > 0
    has_right = me < count - 1
    left = jnp.maximum(me - 1, 0)
    right = jnp.minimum(me + 1, count - 1)
    slow_left = jnp.logical_and(has_left, lax.rem(me, GROUP) == 0)
    slow_right = jnp.logical_and(has_right, lax.rem(me + 1, GROUP) == 0)
    fast_left = jnp.logical_and(has_left, jnp.logical_not(slow_left))
    fast_right = jnp.logical_and(has_right, jnp.logical_not(slow_right))
    first = 2 * core
    two = pl.ds(first, 2)
    tile = power.shape[3:]

    barrier = pltpu.get_barrier_semaphore()

    @pl.when(has_left)
    def _():
        pl.semaphore_signal(barrier, inc=1, device_id={"space": me - 1}, device_id_type=MESH)

    @pl.when(has_right)
    def _():
        pl.semaphore_signal(barrier, inc=1, device_id={"space": me + 1}, device_id_type=MESH)

    pl.semaphore_signal(barrier, inc=1, device_id={"tm": peer}, device_id_type=MESH)

    loads = [
        pltpu.make_async_copy(velocity, raw.at[pl.ds(0, 3), pl.ds(HALO, planes)], local_sem.at[0]),
        pltpu.make_async_copy(diffusivity, raw.at[3, pl.ds(HALO, planes)], local_sem.at[1]),
        pltpu.make_async_copy(initial.at[two], power.at[0, :, pl.ds(EDGE, planes)], local_sem.at[2]),
        pltpu.make_async_copy(weight_rows, weight, local_sem.at[3]),
    ]
    for copy in loads:
        copy.start()

    def clear(first_at, second_at, near_at):
        power[0, :, pl.ds(first_at, W1)] = jnp.zeros((2, W1) + tile, jnp.float32)
        power[W1, :, pl.ds(second_at, W2)] = jnp.zeros((2, W2) + tile, jnp.float32)
        raw[:, pl.ds(near_at, NEAR)] = jnp.zeros((4, NEAR) + tile, jnp.float32)

    @pl.when(jnp.logical_not(has_left))
    def _():
        clear(EDGE - W1, EDGE - W2, HALO - NEAR)

    @pl.when(jnp.logical_not(has_right))
    def _():
        clear(EDGE + planes, EDGE + planes, HALO + planes)

    def remote(side, item, src, dst):
        return pltpu.make_async_remote_copy(
            src_ref=src,
            dst_ref=dst,
            send_sem=send.at[side, item],
            recv_sem=recv.at[side, item],
            device_id={"space": left if side else right},
            device_id_type=MESH,
        )

    def field_halo(side, item, level, t, width):
        src = EDGE if side else EDGE + planes - width
        dst = EDGE + planes if side else EDGE - width
        return remote(side, item, power.at[level, t, pl.ds(src, width)], power.at[level, t, pl.ds(dst, width)])

    def passed(item, side, at, width):
        ref = raw.at[two, pl.ds(at, width)]
        return pltpu.make_async_remote_copy(
            src_ref=ref,
            dst_ref=ref,
            send_sem=pass_send.at[item, side],
            recv_sem=pass_recv.at[item, side],
            device_id={"tm": peer},
            device_id_type=MESH,
        )

    near, first_round, second_round, near_pass = [], [[], []], [[], []], []
    deep, deep_fields, deep_pass = [], [[], []], []
    for side in range(2):
        src = HALO if side else HALO + planes - NEAR
        dst = HALO + planes if side else HALO - NEAR
        near.append(remote(side, 0, raw.at[two, pl.ds(src, NEAR)], raw.at[two, pl.ds(dst, NEAR)]))
        near_pass.append(passed(0, side, dst, NEAR))
        for t in range(2):
            first_round[t].append(field_halo(side, 2 + t, 0, t, W1))
            second_round[t].append(field_halo(side, 4 + t, W1, t, W2))
        src = HALO + NEAR if side else HALO + planes - NEAR - W2
        dst = src + planes if side else src - planes
        deep.append(remote(side, 1, raw.at[two, pl.ds(src, W2)], raw.at[two, pl.ds(dst, W2)]))
        deep_pass.append(passed(1, side, dst, W2))
        src = EDGE + W1 if side else EDGE + planes - W1 - W2
        dst = src + planes if side else src - planes
        for t in range(2):
            deep_fields[t].append(
                remote(side, 6 + t, power.at[0, t, pl.ds(src, W2)], power.at[0, t, pl.ds(dst, W2)])
            )

    def start(to_right, to_left, *pairs):
        for side, there in ((0, to_right), (1, to_left)):

            @pl.when(there)
            def _():
                for pair in pairs:
                    pair[side].start()

    def arrived(from_left, from_right, pair, then=None):
        for side, there in ((0, from_left), (1, from_right)):

            @pl.when(there)
            def _():
                pair[side].wait_recv()
                if then:
                    then[side].start()

    def derive(lo, width):
        for q in [lo + i for i in range(width)]:
            d = DT * raw[3, q]
            for axis in range(3):
                v = (0.5 * DT) * raw[axis, q]
                stencil[2 * axis, q] = d - v
                stencil[2 * axis + 1, q] = d + v
            stencil[6, q] = SHIFT - 6.0 * d

    def advance(t, k, lo, width):
        for q in [lo + i for i in range(width)]:
            c = [stencil[j, q - 1] for j in range(7)]
            u = power[k - 1, t, q]
            x = c[0] * power[k - 1, t, q + 1] + c[1] * power[k - 1, t, q - 1]
            y = c[2] * pltpu.roll(u, u.shape[0] - 1, 0) + c[3] * pltpu.roll(u, 1, 0)
            z = c[4] * pltpu.roll(u, u.shape[1] - 1, 1) + c[5] * pltpu.roll(u, 1, 1)
            power[k, t, q] = (x + y) + (z + c[6] * u)

    def accumulate(t, p, lo, hi, before):
        v = [power[k, t, p + EDGE] for k in range(lo, hi)]
        totals = []
        for j in range(SUMS):
            total = before[j] if before else None
            for k in range(lo, hi):
                term = weight[tm, j * (DEGREE + 1) + k] * v[k - lo]
                total = term if total is None else total + term
            totals.append(total)
        return totals

    for copy in loads:
        copy.wait()
    derive(HALO, planes)

    pl.semaphore_wait(barrier, 1 + has_left.astype(jnp.int32) + has_right.astype(jnp.int32))
    start(has_right, has_left, near, *first_round)

    for side, there in ((0, slow_right), (1, slow_left)):

        @pl.when(there)
        def _():
            near[side].wait_recv()
            deep[side].start()
            near_pass[side].start()
            for t in range(2):
                first_round[t][side].wait_recv()
                deep_fields[t][side].start()

    from_left = jnp.logical_and(has_left, jnp.logical_not(slow_right))
    from_right = jnp.logical_and(has_right, jnp.logical_not(slow_left))
    arrived(from_left, from_right, near, near_pass)
    arrived(has_left, has_right, near_pass)
    derive(HALO - NEAR, NEAR)
    derive(HALO + planes, NEAR)
    for t in range(2):
        arrived(from_left, from_right, first_round[t])
        for k in range(1, W1 + 1):
            advance(t, k, EDGE - W1 + k, planes + 2 * (W1 - k))
        start(fast_right, fast_left, second_round[t])

    for t in range(2):
        for p in range(planes):
            for j, total in enumerate(accumulate(t, p, 0, W1 + 1, None)):
                sums[j, t, p] = total

    arrived(slow_left, slow_right, deep, deep_pass)

    @pl.when(jnp.logical_or(slow_left, slow_right))
    def _():
        arrived(slow_left, slow_right, deep_pass)
        derive(jnp.where(slow_right, HALO + planes + NEAR, HALO - NEAR - W2), W2)
        for t in range(2):
            arrived(slow_left, slow_right, deep_fields[t])
            for k in range(1, W1 + 1):
                advance(t, k, jnp.where(slow_right, EDGE + planes + W1 - k, EDGE - W1 - W2 + k), W2)

    crossings = []
    for t in range(2):
        arrived(fast_left, fast_right, second_round[t])
        for j in range(1, W2 + 1):
            advance(t, W1 + j, EDGE - W2 + j, planes + 2 * (W2 - j))
        for p in range(planes):
            totals = accumulate(t, p, W1 + 1, DEGREE + 1, [sums[j, t, p] for j in range(SUMS)])
            out[2 - 2 * core, first + t, p] = totals[0]
            out[core, first + t, p] = totals[1]
            out[core + 1, first + t, p] = totals[2]
            across[t, 2 * core, p] = totals[0]
            across[t, 1 - core, p] = totals[3]
            across[t, 2 - core, p] = totals[4]
        crossings.append(
            pltpu.make_async_remote_copy(
                src_ref=across.at[t],
                dst_ref=out.at[:, first + t],
                send_sem=cross_send.at[t],
                recv_sem=cross_recv.at[t],
                device_id={"tm": peer},
                device_id_type=MESH,
            )
        )
        crossings[t].start()

    for side, there, fast, slow in ((0, has_right, fast_right, slow_right), (1, has_left, fast_left, slow_left)):

        @pl.when(there)
        def _():
            near[side].wait_send()
            near_pass[1 - side].wait_send()
            for t in range(2):
                first_round[t][side].wait_send()

        @pl.when(fast)
        def _():
            for t in range(2):
                second_round[t][side].wait_send()

        @pl.when(slow)
        def _():
            deep[side].wait_send()
            deep_pass[1 - side].wait_send()
            for t in range(2):
                deep_fields[t][side].wait_send()

    for copy in crossings:
        copy.wait()


def body(initial, velocity, diffusivity):
    planes, rows, lanes = diffusivity.shape
    operands = (jnp.asarray(weights()), initial, velocity, diffusivity)
    nodes = pl.pallas_call(
        functools.partial(kernel, planes),
        out_shape=jax.ShapeDtypeStruct((3,) + initial.shape, jnp.float32),
        in_specs=[pl.BlockSpec(memory_space=pl.ANY)] * 4,
        out_specs=pl.BlockSpec(memory_space=pltpu.VMEM),
        scratch_shapes=[
            pltpu.VMEM((DEGREE + 1, 2, planes + 2 * EDGE, rows, lanes), jnp.float32),
            pltpu.VMEM((4, planes + 2 * HALO, rows, lanes), jnp.float32),
            pltpu.VMEM((7, planes + 2 * HALO, rows, lanes), jnp.float32),
            pltpu.VMEM((SUMS, 2, planes, rows, lanes), jnp.float32),
            pltpu.VMEM((2, 3, planes, rows, lanes), jnp.float32),
            pltpu.SMEM((SLICES, LANES), jnp.float32),
            pltpu.SemaphoreType.DMA((4,)),
            pltpu.SemaphoreType.DMA((2, 8)),
            pltpu.SemaphoreType.DMA((2, 8)),
            pltpu.SemaphoreType.DMA((2, 2)),
            pltpu.SemaphoreType.DMA((2, 2)),
            pltpu.SemaphoreType.DMA((2,)),
            pltpu.SemaphoreType.DMA((2,)),
        ],
        compiler_params=pltpu.CompilerParams(collective_id=0, has_side_effects=True, vmem_limit_bytes=24 * 2**20),
        name="powers",
    )(*[pltpu.with_memory_space_constraint(a, pltpu.HBM) for a in operands])
    return nodes[None]


def solution(mesh):
    return jax.shard_map(
        body,
        mesh=mesh,
        in_specs=(
            P(None, "space", None, None),
            P(None, "space", None, None),
            P("space", None, None),
        ),
        out_specs=P("tm", None, None, "space", None, None),
        check_vma=False,
    )
```

```python
import functools
from fractions import Fraction
from math import comb

import jax
import jax.numpy as jnp
import numpy as np
from jax import lax
from jax.experimental import pallas as pl
from jax.experimental.pallas import tpu as pltpu
from jax.sharding import PartitionSpec as P

SWEEPS = 2
SLICES = 8
DT = 0.25
SHIFT = 0.875
MESH = pl.DeviceIdType.MESH


def combine(*terms):
    total = [Fraction(0)] * max(len(p) for _, p in terms)
    for factor, p in terms:
        for k, a in enumerate(p):
            total[k] += Fraction(factor) * a
    return total


def node_polynomials():
    third, small, large = Fraction(1, 3), Fraction(1, 24), Fraction(5, 24)
    half, sixth = Fraction(1, 2), Fraction(1, 6)
    start = [Fraction(1)]

    def image(p):
        return [Fraction(0)] + list(p)

    guesses = [start]
    for _ in range(SLICES - 1):
        guesses.append(combine((1, guesses[-1]), (1, image(guesses[-1]))))
    nodes = [(g, g, g) for g in guesses]
    fine_ends = None
    for sweep in range(SWEEPS):
        starts = guesses if sweep == 0 else [start] + fine_ends[:-1]
        coarse, new_nodes, new_ends = start, [], []
        for n in range(SLICES):
            s = starts[n]
            o0, o1, o2 = (image(u) for u in nodes[n])
            g0 = image(s)
            m = combine((1, s), (half, g0), (-half, o0), (large, o0), (third, o1), (-small, o2))
            g1 = image(m)
            e = combine((1, m), (half, g1), (-half, o1), (-small, o0), (third, o1), (large, o2))
            g2 = image(e)
            c = combine((sixth, g0), (4 * sixth, g1), (sixth, g2), (-1, g0))
            z = combine((1, coarse), (1, image(coarse)), (1, c))
            middle = combine((1, m), (half, coarse), (-half, s), (half, z), (-half, e))
            new_nodes.append((coarse, middle, z))
            new_ends.append(e)
            coarse = z
        nodes, fine_ends = new_nodes, new_ends
    return nodes


def shifted_powers(p, count):
    c = Fraction(SHIFT)
    out = [Fraction(0)] * max(count, len(p))
    for k, a in enumerate(p):
        for j in range(k + 1):
            out[j] += a * comb(k, j) * (-c) ** (k - j)
    assert not any(out[count:])
    return [float(a) for a in out[:count]]


DEGREE = SLICES - 1 + 3 * SWEEPS
W1 = 7
W2 = DEGREE - W1
EDGE = W1 + W2
HALO = EDGE - 1
NEAR = W1 - 1
SUMS = 5
ROW = 4
LAYER = 16
S1 = 5
S2 = DEGREE - S1
LANES = 128


def weights():
    nodes = node_polynomials()
    table = np.zeros((SLICES, LANES), np.float32)
    for n in range(SLICES):
        a = n - n % 2
        assert nodes[a][2] == nodes[a + 1][0]
        own, other = (nodes[a][:2], nodes[a + 1][1:]) if n == a else (nodes[a + 1][1:], nodes[a][:2])
        row = [shifted_powers(p, DEGREE + 1) for p in (nodes[a][2], *own, *other)]
        table[n, : SUMS * (DEGREE + 1)] = np.reshape(row, -1)
    return table


def kernel(planes, weight_rows, initial, velocity, diffusivity, out, power, raw, stencil, sums, across, landing, weight,
           local_sem, send, recv, pass_send, pass_recv, cross_send, cross_recv):
    count = lax.axis_size("space")
    me = lax.axis_index("space")
    tm = lax.axis_index("tm")
    core = lax.rem(tm, 2)
    peer = tm + 1 - 2 * core
    has_left = me > 0
    has_right = me < count - 1
    left = jnp.maximum(me - 1, 0)
    right = jnp.minimum(me + 1, count - 1)

    def kinds(i, there):
        is_deep = lax.rem(i, LAYER) == 0
        is_late = jnp.logical_and(lax.rem(i, ROW) == 0, jnp.logical_not(is_deep))
        is_fast = jnp.logical_not(jnp.logical_or(is_deep, is_late))
        return [jnp.logical_and(there, kind) for kind in (is_fast, is_late, is_deep)]

    fast_left, late_left, deep_left = kinds(me, has_left)
    fast_right, late_right, deep_right = kinds(me + 1, has_right)
    slow_left = jnp.logical_or(late_left, deep_left)
    slow_right = jnp.logical_or(late_right, deep_right)
    first = 2 * core
    two = pl.ds(first, 2)
    tile = power.shape[3:]

    barrier = pltpu.get_barrier_semaphore()

    @pl.when(has_left)
    def _():
        pl.semaphore_signal(barrier, inc=1, device_id={"space": me - 1}, device_id_type=MESH)

    @pl.when(has_right)
    def _():
        pl.semaphore_signal(barrier, inc=1, device_id={"space": me + 1}, device_id_type=MESH)

    pl.semaphore_signal(barrier, inc=1, device_id={"tm": peer}, device_id_type=MESH)

    loads = [
        pltpu.make_async_copy(velocity, raw.at[pl.ds(0, 3), pl.ds(HALO, planes)], local_sem.at[0]),
        pltpu.make_async_copy(diffusivity, raw.at[3, pl.ds(HALO, planes)], local_sem.at[1]),
        pltpu.make_async_copy(initial.at[two], power.at[0, :, pl.ds(EDGE, planes)], local_sem.at[2]),
        pltpu.make_async_copy(weight_rows, weight, local_sem.at[3]),
    ]
    for copy in loads:
        copy.start()

    def clear(first_at, second_at, near_at):
        power[0, :, pl.ds(first_at, W1)] = jnp.zeros((2, W1) + tile, jnp.float32)
        power[W1, :, pl.ds(second_at, W2)] = jnp.zeros((2, W2) + tile, jnp.float32)
        raw[:, pl.ds(near_at, NEAR)] = jnp.zeros((4, NEAR) + tile, jnp.float32)

    @pl.when(jnp.logical_not(has_left))
    def _():
        clear(EDGE - W1, EDGE - W2, HALO - NEAR)

    @pl.when(jnp.logical_not(has_right))
    def _():
        clear(EDGE + planes, EDGE + planes, HALO + planes)

    def remote(side, item, src, dst):
        return pltpu.make_async_remote_copy(
            src_ref=src,
            dst_ref=dst,
            send_sem=send.at[side, item],
            recv_sem=recv.at[side, item],
            device_id={"space": left if side else right},
            device_id_type=MESH,
        )

    def field_halo(side, item, level, t, width):
        src = EDGE if side else EDGE + planes - width
        dst = EDGE + planes if side else EDGE - width
        return remote(side, item, power.at[level, t, pl.ds(src, width)], power.at[level, t, pl.ds(dst, width)])

    def passed(item, side, at, width):
        ref = raw.at[two, pl.ds(at, width)]
        return pltpu.make_async_remote_copy(
            src_ref=ref,
            dst_ref=ref,
            send_sem=pass_send.at[item, side],
            recv_sem=pass_recv.at[item, side],
            device_id={"tm": peer},
            device_id_type=MESH,
        )

    def coefficient_halo(side, item, src, dst, width):
        return remote(side, item, raw.at[two, pl.ds(src, width)], raw.at[two, pl.ds(dst, width)])

    near, near_pass, first_round, second_round = [], [], [[], []], [[], []]
    near_slow, near_pass_slow, first_slow, second_slow = [], [], [[], []], [[], []]
    far, far_pass = [], []
    deep, deep_pass, deep_fields = [], [], [[], []]
    relay, relay_pass, relay_fields = [], [], [[], []]
    for side in range(2):
        for width, copies, passes in ((NEAR, near, near_pass), (S1 - 1, near_slow, near_pass_slow)):
            src = HALO if side else HALO + planes - width
            dst = HALO + planes if side else HALO - width
            copies.append(coefficient_halo(side, 0, src, dst, width))
            passes.append(passed(0, side, dst, width))
        src = HALO + S1 - 1 if side else HALO + planes - S2 + 1
        dst = src + planes if side else src - planes
        far.append(coefficient_halo(side, 1, src, dst, S2 - S1))
        far_pass.append(passed(1, side, dst, S2 - S1))
        for width, item, skip, copies, passes in (
            (planes - S1 + 1, 1, S1 - 1, deep, deep_pass),
            (DEGREE - 1 - planes, 8, planes, relay, relay_pass),
        ):
            src = HALO + skip if side else HALO + planes - skip - width
            dst = src + planes if side else src - planes
            copies.append(coefficient_halo(side, item, src, dst, width))
            passes.append(passed(1 if item == 1 else 2, side, dst, width))
        for t in range(2):
            first_round[t].append(field_halo(side, 2 + t, 0, t, W1))
            first_slow[t].append(field_halo(side, 2 + t, 0, t, S1))
            second_round[t].append(field_halo(side, 4 + t, W1, t, W2))
            src = EDGE if side else EDGE + planes - S2
            second_slow[t].append(remote(side, 4 + t, power.at[S1, t, pl.ds(src, S2)], landing.at[0, t]))
            for width, item, skip, copies in (
                (planes - S1, 4, S1, deep_fields),
                (DEGREE - planes, 6, planes, relay_fields),
            ):
                src = EDGE + skip if side else EDGE + planes - skip - width
                row = skip - S1 if side else DEGREE - skip - width
                copies[t].append(
                    remote(side, item + t, power.at[0, t, pl.ds(src, width)], landing.at[1, t, pl.ds(row, width)])
                )

    def start(to_right, to_left, *pairs):
        for side, there in ((0, to_right), (1, to_left)):

            @pl.when(there)
            def _():
                for pair in pairs:
                    pair[side].start()

    def arrived(from_left, from_right, pair, then=None):
        for side, there in ((0, from_left), (1, from_right)):

            @pl.when(there)
            def _():
                pair[side].wait_recv()
                if then:
                    then[side].start()

    def derive(lo, width):
        for q in [lo + i for i in range(width)]:
            d = DT * raw[3, q]
            for axis in range(3):
                v = (0.5 * DT) * raw[axis, q]
                stencil[2 * axis, q] = d - v
                stencil[2 * axis + 1, q] = d + v
            stencil[6, q] = SHIFT - 6.0 * d

    def advance(t, k, lo, width):
        for q in [lo + i for i in range(width)]:
            c = [stencil[j, q - 1] for j in range(7)]
            u = power[k - 1, t, q]
            x = c[0] * power[k - 1, t, q + 1] + c[1] * power[k - 1, t, q - 1]
            y = c[2] * pltpu.roll(u, u.shape[0] - 1, 0) + c[3] * pltpu.roll(u, 1, 0)
            z = c[4] * pltpu.roll(u, u.shape[1] - 1, 1) + c[5] * pltpu.roll(u, 1, 1)
            power[k, t, q] = (x + y) + (z + c[6] * u)

    def accumulate(t, p, lo, hi, before):
        v = [power[k, t, p + EDGE] for k in range(lo, hi)]
        totals = []
        for j in range(SUMS):
            total = before[j] if before else None
            for k in range(lo, hi):
                term = weight[tm, j * (DEGREE + 1) + k] * v[k - lo]
                total = term if total is None else total + term
            totals.append(total)
        return totals

    for copy in loads:
        copy.wait()
    derive(HALO, planes)

    pl.semaphore_wait(barrier, 1 + has_left.astype(jnp.int32) + has_right.astype(jnp.int32))
    start(slow_right, slow_left, near_slow, *first_slow)
    start(fast_right, fast_left, near, *first_round)
    start(deep_right, deep_left, deep, *deep_fields)

    for side, there in ((0, deep_right), (1, deep_left)):

        @pl.when(there)
        def _():
            near[side].wait_recv()
            relay[side].start()
            near_pass[side].start()
            for t in range(2):
                first_round[t][side].wait_recv()
                relay_fields[t][side].start()

    from_left = jnp.logical_and(fast_left, jnp.logical_not(deep_right))
    from_right = jnp.logical_and(fast_right, jnp.logical_not(deep_left))
    arrived(from_left, from_right, near, near_pass)
    arrived(slow_left, slow_right, near_slow, near_pass_slow)
    start(late_right, late_left, far)
    arrived(fast_left, fast_right, near_pass)
    arrived(slow_left, slow_right, near_pass_slow)
    derive(HALO - S1 + 1, S1 - 1)
    derive(HALO + planes, S1 - 1)

    @pl.when(jnp.logical_not(slow_left))
    def _():
        derive(HALO - NEAR, NEAR - S1 + 1)

    @pl.when(jnp.logical_not(slow_right))
    def _():
        derive(HALO + planes + S1 - 1, NEAR - S1 + 1)

    for t in range(2):
        arrived(from_left, from_right, first_round[t])
        arrived(slow_left, slow_right, first_slow[t])
        for k in range(1, W1 + 1):
            advance(t, k, EDGE - W1 + k, planes + 2 * (W1 - k))
            if k == S1:
                start(late_right, late_left, second_slow[t])
        start(fast_right, fast_left, second_round[t])

    for t in range(2):
        for p in range(planes):
            for j, total in enumerate(accumulate(t, p, 0, S1 + 1, None)):
                sums[j, t, p] = total

    arrived(late_left, late_right, far, far_pass)
    arrived(deep_left, deep_right, deep, deep_pass)
    arrived(deep_left, deep_right, relay, relay_pass)

    for side, late, far_off in ((0, late_left, deep_left), (1, late_right, deep_right)):
        for there, arrivals, width in ((late, [far_pass], S2 - S1), (far_off, [deep_pass, relay_pass], S2)):

            @pl.when(there)
            def _():
                for passes in arrivals:
                    passes[side].wait_recv()
                derive(HALO + planes + S1 - 1 if side else HALO - S1 + 1 - width, width)

    def outer(side, k):
        return EDGE + planes + S1 - k if side else EDGE - DEGREE + k

    for side, far_off in ((0, deep_left), (1, deep_right)):

        @pl.when(far_off)
        def _():
            for t in range(2):
                deep_fields[t][side].wait_recv()
                relay_fields[t][side].wait_recv()
                for i in range(S2):
                    power[0, t, outer(side, 0) + i] = landing[1, t, i]
            for k in range(1, W1 + 1):
                for t in range(2):
                    advance(t, k, outer(side, k), S2)

    def widen(t):
        for side, late in ((0, late_left), (1, late_right)):

            @pl.when(late)
            def _():
                second_slow[t][side].wait_recv()
                for i in range(S2):
                    power[S1, t, outer(side, S1) + i] = landing[0, t, i]
                for k in range(S1 + 1, W1 + 1):
                    advance(t, k, outer(side, k), S2)

    crossings = []
    for t in range(2):
        widen(t)
        arrived(fast_left, fast_right, second_round[t])
        for j in range(1, W2 + 1):
            advance(t, W1 + j, EDGE - W2 + j, planes + 2 * (W2 - j))
        for p in range(planes):
            totals = accumulate(t, p, S1 + 1, DEGREE + 1, [sums[j, t, p] for j in range(SUMS)])
            out[2 - 2 * core, first + t, p] = totals[0]
            out[core, first + t, p] = totals[1]
            out[core + 1, first + t, p] = totals[2]
            across[t, 2 * core, p] = totals[0]
            across[t, 1 - core, p] = totals[3]
            across[t, 2 - core, p] = totals[4]
        crossings.append(
            pltpu.make_async_remote_copy(
                src_ref=across.at[t],
                dst_ref=out.at[:, first + t],
                send_sem=cross_send.at[t],
                recv_sem=cross_recv.at[t],
                device_id={"tm": peer},
                device_id_type=MESH,
            )
        )
        crossings[t].start()

    sides = (
        (0, fast_right, slow_right, late_right, deep_right),
        (1, fast_left, slow_left, late_left, deep_left),
    )
    for side, fast, slow, late, far_off in sides:
        for there, copies, passes in (
            (fast, [near, *first_round, *second_round], [near_pass]),
            (slow, [near_slow, *first_slow], [near_pass_slow]),
            (late, [far, *second_slow], [far_pass]),
            (far_off, [deep, relay, *deep_fields, *relay_fields], [deep_pass, relay_pass]),
        ):

            @pl.when(there)
            def _():
                for copy in copies:
                    copy[side].wait_send()
                for handed in passes:
                    handed[1 - side].wait_send()

    for copy in crossings:
        copy.wait()


def body(initial, velocity, diffusivity):
    planes, rows, lanes = diffusivity.shape
    operands = (jnp.asarray(weights()), initial, velocity, diffusivity)
    nodes = pl.pallas_call(
        functools.partial(kernel, planes),
        out_shape=jax.ShapeDtypeStruct((3,) + initial.shape, jnp.float32),
        in_specs=[pl.BlockSpec(memory_space=pl.ANY)] * 4,
        out_specs=pl.BlockSpec(memory_space=pltpu.VMEM),
        scratch_shapes=[
            pltpu.VMEM((DEGREE + 1, 2, planes + 2 * EDGE, rows, lanes), jnp.float32),
            pltpu.VMEM((4, planes + 2 * HALO, rows, lanes), jnp.float32),
            pltpu.VMEM((7, planes + 2 * HALO, rows, lanes), jnp.float32),
            pltpu.VMEM((SUMS, 2, planes, rows, lanes), jnp.float32),
            pltpu.VMEM((2, 3, planes, rows, lanes), jnp.float32),
            pltpu.VMEM((2, 2, S2, rows, lanes), jnp.float32),
            pltpu.SMEM((SLICES, LANES), jnp.float32),
            pltpu.SemaphoreType.DMA((4,)),
            pltpu.SemaphoreType.DMA((2, 9)),
            pltpu.SemaphoreType.DMA((2, 9)),
            pltpu.SemaphoreType.DMA((3, 2)),
            pltpu.SemaphoreType.DMA((3, 2)),
            pltpu.SemaphoreType.DMA((2,)),
            pltpu.SemaphoreType.DMA((2,)),
        ],
        compiler_params=pltpu.CompilerParams(collective_id=0, has_side_effects=True, vmem_limit_bytes=24 * 2**20),
        name="powers",
    )(*[pltpu.with_memory_space_constraint(a, pltpu.HBM) for a in operands])
    return nodes[None]


def solution(mesh):
    return jax.shard_map(
        body,
        mesh=mesh,
        in_specs=(
            P(None, "space", None, None),
            P(None, "space", None, None),
            P("space", None, None),
        ),
        out_specs=P("tm", None, None, "space", None, None),
        check_vma=False,
    )
```

```python
import functools
from fractions import Fraction
from math import comb

import jax
import jax.numpy as jnp
import numpy as np
from jax import lax
from jax.experimental import pallas as pl
from jax.experimental.pallas import tpu as pltpu
from jax.sharding import PartitionSpec as P

SWEEPS = 2
SLICES = 8
DT = 0.25
SHIFT = 0.875
MESH = pl.DeviceIdType.MESH


def combine(*terms):
    total = [Fraction(0)] * max(len(p) for _, p in terms)
    for factor, p in terms:
        for k, a in enumerate(p):
            total[k] += Fraction(factor) * a
    return total


def node_polynomials():
    third, small, large = Fraction(1, 3), Fraction(1, 24), Fraction(5, 24)
    half, sixth = Fraction(1, 2), Fraction(1, 6)
    start = [Fraction(1)]

    def image(p):
        return [Fraction(0)] + list(p)

    guesses = [start]
    for _ in range(SLICES - 1):
        guesses.append(combine((1, guesses[-1]), (1, image(guesses[-1]))))
    nodes = [(g, g, g) for g in guesses]
    fine_ends = None
    for sweep in range(SWEEPS):
        starts = guesses if sweep == 0 else [start] + fine_ends[:-1]
        coarse, new_nodes, new_ends = start, [], []
        for n in range(SLICES):
            s = starts[n]
            o0, o1, o2 = (image(u) for u in nodes[n])
            g0 = image(s)
            m = combine((1, s), (half, g0), (-half, o0), (large, o0), (third, o1), (-small, o2))
            g1 = image(m)
            e = combine((1, m), (half, g1), (-half, o1), (-small, o0), (third, o1), (large, o2))
            g2 = image(e)
            c = combine((sixth, g0), (4 * sixth, g1), (sixth, g2), (-1, g0))
            z = combine((1, coarse), (1, image(coarse)), (1, c))
            middle = combine((1, m), (half, coarse), (-half, s), (half, z), (-half, e))
            new_nodes.append((coarse, middle, z))
            new_ends.append(e)
            coarse = z
        nodes, fine_ends = new_nodes, new_ends
    return nodes


def shifted_powers(p, count):
    c = Fraction(SHIFT)
    out = [Fraction(0)] * max(count, len(p))
    for k, a in enumerate(p):
        for j in range(k + 1):
            out[j] += a * comb(k, j) * (-c) ** (k - j)
    assert not any(out[count:])
    return [float(a) for a in out[:count]]


DEGREE = SLICES - 1 + 3 * SWEEPS
W1 = 7
W2 = DEGREE - W1
EDGE = W1 + W2
HALO = EDGE - 1
NEAR = W1 - 1
SUMS = 5
ROW = 4
LAYER = 16
S1 = 5
S2 = DEGREE - S1
LANES = 128


def weights():
    nodes = node_polynomials()
    table = np.zeros((SLICES, LANES), np.float32)
    for n in range(SLICES):
        a = n - n % 2
        assert nodes[a][2] == nodes[a + 1][0]
        own, other = (nodes[a][:2], nodes[a + 1][1:]) if n == a else (nodes[a + 1][1:], nodes[a][:2])
        row = [shifted_powers(p, DEGREE + 1) for p in (nodes[a][2], *own, *other)]
        table[n, : SUMS * (DEGREE + 1)] = np.reshape(row, -1)
    return table


def kernel(planes, weight_rows, initial, velocity, diffusivity, out, power, raw, stencil, sums, across, landing, weight,
           local_sem, send, recv, pass_send, pass_recv, cross_send, cross_recv):
    count = lax.axis_size("space")
    me = lax.axis_index("space")
    tm = lax.axis_index("tm")
    core = lax.rem(tm, 2)
    peer = tm + 1 - 2 * core
    has_left = me > 0
    has_right = me < count - 1
    left = jnp.maximum(me - 1, 0)
    right = jnp.minimum(me + 1, count - 1)

    def kinds(i, there):
        is_deep = lax.rem(i, LAYER) == 0
        is_late = jnp.logical_and(lax.rem(i, ROW) == 0, jnp.logical_not(is_deep))
        is_fast = jnp.logical_not(jnp.logical_or(is_deep, is_late))
        return [jnp.logical_and(there, kind) for kind in (is_fast, is_late, is_deep)]

    fast_left, late_left, deep_left = kinds(me, has_left)
    fast_right, late_right, deep_right = kinds(me + 1, has_right)
    slow_left = jnp.logical_or(late_left, deep_left)
    slow_right = jnp.logical_or(late_right, deep_right)
    first = 2 * core
    two = pl.ds(first, 2)
    tile = power.shape[3:]

    barrier = pltpu.get_barrier_semaphore()

    @pl.when(has_left)
    def _():
        pl.semaphore_signal(barrier, inc=1, device_id={"space": me - 1}, device_id_type=MESH)

    @pl.when(has_right)
    def _():
        pl.semaphore_signal(barrier, inc=1, device_id={"space": me + 1}, device_id_type=MESH)

    pl.semaphore_signal(barrier, inc=1, device_id={"tm": peer}, device_id_type=MESH)

    loads = [
        pltpu.make_async_copy(velocity, raw.at[pl.ds(0, 3), pl.ds(HALO, planes)], local_sem.at[0]),
        pltpu.make_async_copy(diffusivity, raw.at[3, pl.ds(HALO, planes)], local_sem.at[1]),
        pltpu.make_async_copy(initial.at[two], power.at[0, :, pl.ds(EDGE, planes)], local_sem.at[2]),
        pltpu.make_async_copy(weight_rows, weight, local_sem.at[3]),
    ]
    for copy in loads:
        copy.start()

    def clear(first_at, second_at, near_at):
        power[0, :, pl.ds(first_at, W1)] = jnp.zeros((2, W1) + tile, jnp.float32)
        power[W1, :, pl.ds(second_at, W2)] = jnp.zeros((2, W2) + tile, jnp.float32)
        raw[:, pl.ds(near_at, NEAR)] = jnp.zeros((4, NEAR) + tile, jnp.float32)

    @pl.when(jnp.logical_not(has_left))
    def _():
        clear(EDGE - W1, EDGE - W2, HALO - NEAR)

    @pl.when(jnp.logical_not(has_right))
    def _():
        clear(EDGE + planes, EDGE + planes, HALO + planes)

    def remote(side, item, src, dst):
        return pltpu.make_async_remote_copy(
            src_ref=src,
            dst_ref=dst,
            send_sem=send.at[side, item],
            recv_sem=recv.at[side, item],
            device_id={"space": left if side else right},
            device_id_type=MESH,
        )

    def field_halo(side, item, level, t, width):
        src = EDGE if side else EDGE + planes - width
        dst = EDGE + planes if side else EDGE - width
        return remote(side, item, power.at[level, t, pl.ds(src, width)], power.at[level, t, pl.ds(dst, width)])

    def passed(item, side, at, width):
        ref = raw.at[two, pl.ds(at, width)]
        return pltpu.make_async_remote_copy(
            src_ref=ref,
            dst_ref=ref,
            send_sem=pass_send.at[item, side],
            recv_sem=pass_recv.at[item, side],
            device_id={"tm": peer},
            device_id_type=MESH,
        )

    def coefficient_halo(side, item, src, dst, width):
        return remote(side, item, raw.at[two, pl.ds(src, width)], raw.at[two, pl.ds(dst, width)])

    near, near_pass, first_round, second_round = [], [], [[], []], [[], []]
    near_slow, near_pass_slow, first_slow, second_slow = [], [], [[], []], [[], []]
    far, far_pass = [], []
    deep, deep_pass, deep_fields = [], [], [[], []]
    relay, relay_pass, relay_fields = [], [], [[], []]
    for side in range(2):
        for width, copies, passes in ((NEAR, near, near_pass), (S1 - 1, near_slow, near_pass_slow)):
            src = HALO if side else HALO + planes - width
            dst = HALO + planes if side else HALO - width
            copies.append(coefficient_halo(side, 0, src, dst, width))
            passes.append(passed(0, side, dst, width))
        src = HALO + S1 - 1 if side else HALO + planes - S2 + 1
        dst = src + planes if side else src - planes
        far.append(coefficient_halo(side, 1, src, dst, S2 - S1))
        far_pass.append(passed(1, side, dst, S2 - S1))
        for width, item, skip, copies, passes in (
            (planes - S1 + 1, 1, S1 - 1, deep, deep_pass),
            (DEGREE - 1 - planes, 8, planes, relay, relay_pass),
        ):
            src = HALO + skip if side else HALO + planes - skip - width
            dst = src + planes if side else src - planes
            copies.append(coefficient_halo(side, item, src, dst, width))
            passes.append(passed(1 if item == 1 else 2, side, dst, width))
        for t in range(2):
            first_round[t].append(field_halo(side, 2 + t, 0, t, W1))
            first_slow[t].append(field_halo(side, 2 + t, 0, t, S1))
            second_round[t].append(field_halo(side, 4 + t, W1, t, W2))
            src = EDGE if side else EDGE + planes - S2
            second_slow[t].append(remote(side, 4 + t, power.at[S1, t, pl.ds(src, S2)], landing.at[0, t]))
            for width, item, skip, copies in (
                (planes - S1, 4, S1, deep_fields),
                (DEGREE - planes, 6, planes, relay_fields),
            ):
                src = EDGE + skip if side else EDGE + planes - skip - width
                row = skip - S1 if side else DEGREE - skip - width
                copies[t].append(
                    remote(side, item + t, power.at[0, t, pl.ds(src, width)], landing.at[1, t, pl.ds(row, width)])
                )

    def start(to_right, to_left, *pairs):
        for side, there in ((0, to_right), (1, to_left)):

            @pl.when(there)
            def _():
                for pair in pairs:
                    pair[side].start()

    def arrived(from_left, from_right, pair, then=None):
        for side, there in ((0, from_left), (1, from_right)):

            @pl.when(there)
            def _():
                pair[side].wait_recv()
                if then:
                    then[side].start()

    def derive(lo, width):
        for q in [lo + i for i in range(width)]:
            d = DT * raw[3, q]
            for axis in range(3):
                v = (0.5 * DT) * raw[axis, q]
                stencil[2 * axis, q] = d - v
                stencil[2 * axis + 1, q] = d + v
            stencil[6, q] = SHIFT - 6.0 * d

    def advance(t, k, lo, width):
        for q in [lo + i for i in range(width)]:
            c = [stencil[j, q - 1] for j in range(7)]
            u = power[k - 1, t, q]
            x = c[0] * power[k - 1, t, q + 1] + c[1] * power[k - 1, t, q - 1]
            y = c[2] * pltpu.roll(u, u.shape[0] - 1, 0) + c[3] * pltpu.roll(u, 1, 0)
            z = c[4] * pltpu.roll(u, u.shape[1] - 1, 1) + c[5] * pltpu.roll(u, 1, 1)
            power[k, t, q] = (x + y) + (z + c[6] * u)

    def accumulate(t, p, lo, hi, before):
        v = [power[k, t, p + EDGE] for k in range(lo, hi)]
        totals = []
        for j in range(SUMS):
            total = before[j] if before else None
            for k in range(lo, hi):
                term = weight[tm, j * (DEGREE + 1) + k] * v[k - lo]
                total = term if total is None else total + term
            totals.append(total)
        return totals

    for copy in loads:
        copy.wait()
    derive(HALO, planes)

    pl.semaphore_wait(barrier, 1 + has_left.astype(jnp.int32) + has_right.astype(jnp.int32))
    start(slow_right, slow_left, near_slow, *first_slow)
    start(fast_right, fast_left, near, *first_round)

    @pl.when(deep_right)
    def _():
        deep[0].start()
        deep_fields[0][0].start()

    for side, there in ((0, deep_right), (1, deep_left)):

        @pl.when(there)
        def _():
            near[side].wait_recv()
            near_pass[side].start()
            if side:
                deep[side].start()
                deep_fields[0][side].start()
            relay[side].start()
            first_round[0][side].wait_recv()
            relay_fields[0][side].start()
            first_round[1][side].wait_recv()
            if not side:
                relay_fields[0][side].wait_send()
                deep_fields[1][side].start()
                relay_fields[1][side].start()

    from_left = jnp.logical_and(fast_left, jnp.logical_not(deep_right))
    from_right = jnp.logical_and(fast_right, jnp.logical_not(deep_left))
    arrived(from_left, from_right, near, near_pass)
    arrived(slow_left, slow_right, near_slow, near_pass_slow)
    start(late_right, late_left, far)
    arrived(fast_left, fast_right, near_pass)
    arrived(slow_left, slow_right, near_pass_slow)
    derive(HALO - S1 + 1, S1 - 1)
    derive(HALO + planes, S1 - 1)

    @pl.when(jnp.logical_not(slow_left))
    def _():
        derive(HALO - NEAR, NEAR - S1 + 1)

    @pl.when(jnp.logical_not(slow_right))
    def _():
        derive(HALO + planes + S1 - 1, NEAR - S1 + 1)

    for t in range(2):
        arrived(from_left, from_right, first_round[t])
        arrived(slow_left, slow_right, first_slow[t])
        for k in range(1, W1 + 1):
            advance(t, k, EDGE - W1 + k, planes + 2 * (W1 - k))
            if k == S1:
                start(late_right, late_left, second_slow[t])
        start(fast_right, fast_left, second_round[t])
        if t == 0:

            @pl.when(deep_left)
            def _():
                deep_fields[1][1].start()
                relay_fields[1][1].start()


    for t in range(2):
        for p in range(planes):
            for j, total in enumerate(accumulate(t, p, 0, S1 + 1, None)):
                sums[j, t, p] = total

    arrived(late_left, late_right, far, far_pass)
    arrived(deep_left, deep_right, deep, deep_pass)
    arrived(deep_left, deep_right, relay, relay_pass)

    for side, late, far_off in ((0, late_left, deep_left), (1, late_right, deep_right)):
        for there, arrivals, width in ((late, [far_pass], S2 - S1), (far_off, [deep_pass, relay_pass], S2)):

            @pl.when(there)
            def _():
                for passes in arrivals:
                    passes[side].wait_recv()
                derive(HALO + planes + S1 - 1 if side else HALO - S1 + 1 - width, width)

    def outer(side, k):
        return EDGE + planes + S1 - k if side else EDGE - DEGREE + k

    def widen(t):
        for side, late, far_off in ((0, late_left, deep_left), (1, late_right, deep_right)):

            @pl.when(far_off)
            def _():
                deep_fields[t][side].wait_recv()
                relay_fields[t][side].wait_recv()
                for i in range(S2):
                    power[0, t, outer(side, 0) + i] = landing[1, t, i]
                for k in range(1, W1 + 1):
                    advance(t, k, outer(side, k), S2)

            @pl.when(late)
            def _():
                second_slow[t][side].wait_recv()
                for i in range(S2):
                    power[S1, t, outer(side, S1) + i] = landing[0, t, i]
                for k in range(S1 + 1, W1 + 1):
                    advance(t, k, outer(side, k), S2)

    crossings = []
    for t in range(2):
        widen(t)
        arrived(fast_left, fast_right, second_round[t])
        for j in range(1, W2 + 1):
            advance(t, W1 + j, EDGE - W2 + j, planes + 2 * (W2 - j))
        for p in range(planes):
            totals = accumulate(t, p, S1 + 1, DEGREE + 1, [sums[j, t, p] for j in range(SUMS)])
            out[2 - 2 * core, first + t, p] = totals[0]
            out[core, first + t, p] = totals[1]
            out[core + 1, first + t, p] = totals[2]
            across[t, 2 * core, p] = totals[0]
            across[t, 1 - core, p] = totals[3]
            across[t, 2 - core, p] = totals[4]
        crossings.append(
            pltpu.make_async_remote_copy(
                src_ref=across.at[t],
                dst_ref=out.at[:, first + t],
                send_sem=cross_send.at[t],
                recv_sem=cross_recv.at[t],
                device_id={"tm": peer},
                device_id_type=MESH,
            )
        )
        crossings[t].start()

    sides = (
        (0, fast_right, slow_right, late_right, deep_right),
        (1, fast_left, slow_left, late_left, deep_left),
    )
    for side, fast, slow, late, far_off in sides:
        for there, copies, passes in (
            (fast, [near, *first_round, *second_round], [near_pass]),
            (slow, [near_slow, *first_slow], [near_pass_slow]),
            (late, [far, *second_slow], [far_pass]),
            (far_off, [deep, relay, *deep_fields, *relay_fields], [deep_pass, relay_pass]),
        ):

            @pl.when(there)
            def _():
                for copy in copies:
                    if side or copy is not relay_fields[0]:
                        copy[side].wait_send()
                for handed in passes:
                    handed[1 - side].wait_send()

    for copy in crossings:
        copy.wait()


def body(initial, velocity, diffusivity):
    planes, rows, lanes = diffusivity.shape
    operands = (jnp.asarray(weights()), initial, velocity, diffusivity)
    nodes = pl.pallas_call(
        functools.partial(kernel, planes),
        out_shape=jax.ShapeDtypeStruct((3,) + initial.shape, jnp.float32),
        in_specs=[pl.BlockSpec(memory_space=pl.ANY)] * 4,
        out_specs=pl.BlockSpec(memory_space=pltpu.VMEM),
        scratch_shapes=[
            pltpu.VMEM((DEGREE + 1, 2, planes + 2 * EDGE, rows, lanes), jnp.float32),
            pltpu.VMEM((4, planes + 2 * HALO, rows, lanes), jnp.float32),
            pltpu.VMEM((7, planes + 2 * HALO, rows, lanes), jnp.float32),
            pltpu.VMEM((SUMS, 2, planes, rows, lanes), jnp.float32),
            pltpu.VMEM((2, 3, planes, rows, lanes), jnp.float32),
            pltpu.VMEM((2, 2, S2, rows, lanes), jnp.float32),
            pltpu.SMEM((SLICES, LANES), jnp.float32),
            pltpu.SemaphoreType.DMA((4,)),
            pltpu.SemaphoreType.DMA((2, 9)),
            pltpu.SemaphoreType.DMA((2, 9)),
            pltpu.SemaphoreType.DMA((3, 2)),
            pltpu.SemaphoreType.DMA((3, 2)),
            pltpu.SemaphoreType.DMA((2,)),
            pltpu.SemaphoreType.DMA((2,)),
        ],
        compiler_params=pltpu.CompilerParams(collective_id=0, has_side_effects=True, vmem_limit_bytes=24 * 2**20),
        name="powers",
    )(*[pltpu.with_memory_space_constraint(a, pltpu.HBM) for a in operands])
    return nodes[None]


def solution(mesh):
    return jax.shard_map(
        body,
        mesh=mesh,
        in_specs=(
            P(None, "space", None, None),
            P(None, "space", None, None),
            P("space", None, None),
        ),
        out_specs=P("tm", None, None, "space", None, None),
        check_vma=False,
    )
```

```python
import functools
from fractions import Fraction
from math import comb

import jax
import jax.numpy as jnp
import numpy as np
from jax import lax
from jax.experimental import pallas as pl
from jax.experimental.pallas import tpu as pltpu
from jax.sharding import PartitionSpec as P

SWEEPS = 2
SLICES = 8
DT = 0.25
SHIFT = 0.875
MESH = pl.DeviceIdType.MESH


def combine(*terms):
    total = [Fraction(0)] * max(len(p) for _, p in terms)
    for factor, p in terms:
        for k, a in enumerate(p):
            total[k] += Fraction(factor) * a
    return total


def node_polynomials():
    third, small, large = Fraction(1, 3), Fraction(1, 24), Fraction(5, 24)
    half, sixth = Fraction(1, 2), Fraction(1, 6)
    start = [Fraction(1)]

    def image(p):
        return [Fraction(0)] + list(p)

    guesses = [start]
    for _ in range(SLICES - 1):
        guesses.append(combine((1, guesses[-1]), (1, image(guesses[-1]))))
    nodes = [(g, g, g) for g in guesses]
    fine_ends = None
    for sweep in range(SWEEPS):
        starts = guesses if sweep == 0 else [start] + fine_ends[:-1]
        coarse, new_nodes, new_ends = start, [], []
        for n in range(SLICES):
            s = starts[n]
            o0, o1, o2 = (image(u) for u in nodes[n])
            g0 = image(s)
            m = combine((1, s), (half, g0), (-half, o0), (large, o0), (third, o1), (-small, o2))
            g1 = image(m)
            e = combine((1, m), (half, g1), (-half, o1), (-small, o0), (third, o1), (large, o2))
            g2 = image(e)
            c = combine((sixth, g0), (4 * sixth, g1), (sixth, g2), (-1, g0))
            z = combine((1, coarse), (1, image(coarse)), (1, c))
            middle = combine((1, m), (half, coarse), (-half, s), (half, z), (-half, e))
            new_nodes.append((coarse, middle, z))
            new_ends.append(e)
            coarse = z
        nodes, fine_ends = new_nodes, new_ends
    return nodes


def shifted_powers(p, count):
    c = Fraction(SHIFT)
    out = [Fraction(0)] * max(count, len(p))
    for k, a in enumerate(p):
        for j in range(k + 1):
            out[j] += a * comb(k, j) * (-c) ** (k - j)
    assert not any(out[count:])
    return [float(a) for a in out[:count]]


DEGREE = SLICES - 1 + 3 * SWEEPS
W1 = 7
W2 = DEGREE - W1
EDGE = W1 + W2
HALO = EDGE - 1
NEAR = W1 - 1
SUMS = 5
ROW = 4
LAYER = 16
S1 = 5
S2 = DEGREE - S1
LANES = 128


def weights():
    nodes = node_polynomials()
    table = np.zeros((SLICES, LANES), np.float32)
    for n in range(SLICES):
        a = n - n % 2
        assert nodes[a][2] == nodes[a + 1][0]
        own, other = (nodes[a][:2], nodes[a + 1][1:]) if n == a else (nodes[a + 1][1:], nodes[a][:2])
        row = [shifted_powers(p, DEGREE + 1) for p in (nodes[a][2], *own, *other)]
        table[n, : SUMS * (DEGREE + 1)] = np.reshape(row, -1)
    return table


def kernel(planes, weight_rows, initial, velocity, diffusivity, out, power, raw, stencil, sums, across, landing, weight,
           local_sem, send, recv, pass_send, pass_recv, cross_send, cross_recv):
    count = lax.axis_size("space")
    me = lax.axis_index("space")
    tm = lax.axis_index("tm")
    core = lax.rem(tm, 2)
    peer = tm + 1 - 2 * core
    has_left = me > 0
    has_right = me < count - 1
    left = jnp.maximum(me - 1, 0)
    right = jnp.minimum(me + 1, count - 1)

    def kinds(i, there):
        is_deep = lax.rem(i, LAYER) == 0
        is_late = jnp.logical_and(lax.rem(i, ROW) == 0, jnp.logical_not(is_deep))
        is_fast = jnp.logical_not(jnp.logical_or(is_deep, is_late))
        return [jnp.logical_and(there, kind) for kind in (is_fast, is_late, is_deep)]

    fast_left, late_left, deep_left = kinds(me, has_left)
    fast_right, late_right, deep_right = kinds(me + 1, has_right)
    slow_left = jnp.logical_or(late_left, deep_left)
    slow_right = jnp.logical_or(late_right, deep_right)
    first = 2 * core
    two = pl.ds(first, 2)
    tile = power.shape[3:]

    barrier = pltpu.get_barrier_semaphore()

    @pl.when(has_left)
    def _():
        pl.semaphore_signal(barrier, inc=1, device_id={"space": me - 1}, device_id_type=MESH)

    @pl.when(has_right)
    def _():
        pl.semaphore_signal(barrier, inc=1, device_id={"space": me + 1}, device_id_type=MESH)

    pl.semaphore_signal(barrier, inc=1, device_id={"tm": peer}, device_id_type=MESH)

    loads = [
        pltpu.make_async_copy(velocity, raw.at[pl.ds(0, 3), pl.ds(HALO, planes)], local_sem.at[0]),
        pltpu.make_async_copy(diffusivity, raw.at[3, pl.ds(HALO, planes)], local_sem.at[1]),
        pltpu.make_async_copy(initial.at[two], power.at[0, :, pl.ds(EDGE, planes)], local_sem.at[2]),
        pltpu.make_async_copy(weight_rows, weight, local_sem.at[3]),
    ]
    for copy in loads:
        copy.start()

    def clear(first_at, second_at, near_at):
        power[0, :, pl.ds(first_at, W1)] = jnp.zeros((2, W1) + tile, jnp.float32)
        power[W1, :, pl.ds(second_at, W2)] = jnp.zeros((2, W2) + tile, jnp.float32)
        raw[:, pl.ds(near_at, NEAR)] = jnp.zeros((4, NEAR) + tile, jnp.float32)

    @pl.when(jnp.logical_not(has_left))
    def _():
        clear(EDGE - W1, EDGE - W2, HALO - NEAR)

    @pl.when(jnp.logical_not(has_right))
    def _():
        clear(EDGE + planes, EDGE + planes, HALO + planes)

    def remote(side, item, src, dst):
        return pltpu.make_async_remote_copy(
            src_ref=src,
            dst_ref=dst,
            send_sem=send.at[side, item],
            recv_sem=recv.at[side, item],
            device_id={"space": left if side else right},
            device_id_type=MESH,
        )

    def field_halo(side, item, level, t, width):
        src = EDGE if side else EDGE + planes - width
        dst = EDGE + planes if side else EDGE - width
        return remote(side, item, power.at[level, t, pl.ds(src, width)], power.at[level, t, pl.ds(dst, width)])

    def passed(item, side, at, width):
        ref = raw.at[two, pl.ds(at, width)]
        return pltpu.make_async_remote_copy(
            src_ref=ref,
            dst_ref=ref,
            send_sem=pass_send.at[item, side],
            recv_sem=pass_recv.at[item, side],
            device_id={"tm": peer},
            device_id_type=MESH,
        )

    def coefficient_halo(side, item, src, dst, width):
        return remote(side, item, raw.at[two, pl.ds(src, width)], raw.at[two, pl.ds(dst, width)])

    near, near_pass, first_round, second_round = [], [], [[], []], [[], []]
    near_slow, near_pass_slow, first_slow, second_slow = [], [], [[], []], [[], []]
    far, far_pass = [], []
    deep, deep_pass, deep_fields = [], [], [[], []]
    relay, relay_pass, relay_fields = [], [], [[], []]
    for side in range(2):
        for width, copies, passes in ((NEAR, near, near_pass), (S1 - 1, near_slow, near_pass_slow)):
            src = HALO if side else HALO + planes - width
            dst = HALO + planes if side else HALO - width
            copies.append(coefficient_halo(side, 0, src, dst, width))
            passes.append(passed(0, side, dst, width))
        src = HALO + S1 - 1 if side else HALO + planes - S2 + 1
        dst = src + planes if side else src - planes
        far.append(coefficient_halo(side, 1, src, dst, S2 - S1))
        far_pass.append(passed(1, side, dst, S2 - S1))
        for width, item, skip, copies, passes in (
            (planes - S1 + 1, 1, S1 - 1, deep, deep_pass),
            (DEGREE - 1 - planes, 8, planes, relay, relay_pass),
        ):
            src = HALO + skip if side else HALO + planes - skip - width
            dst = src + planes if side else src - planes
            copies.append(coefficient_halo(side, item, src, dst, width))
            passes.append(passed(1 if item == 1 else 2, side, dst, width))
        for t in range(2):
            first_round[t].append(field_halo(side, 2 + t, 0, t, W1))
            first_slow[t].append(field_halo(side, 2 + t, 0, t, S1))
            second_round[t].append(field_halo(side, 4 + t, W1, t, W2))
            src = EDGE if side else EDGE + planes - S2
            second_slow[t].append(remote(side, 4 + t, power.at[S1, t, pl.ds(src, S2)], landing.at[0, t]))
            for width, item, skip, copies in (
                (planes - S1, 4, S1, deep_fields),
                (DEGREE - planes, 6, planes, relay_fields),
            ):
                src = EDGE + skip if side else EDGE + planes - skip - width
                row = skip - S1 if side else DEGREE - skip - width
                copies[t].append(
                    remote(side, item + t, power.at[0, t, pl.ds(src, width)], landing.at[1, t, pl.ds(row, width)])
                )

    def start(to_right, to_left, *pairs):
        for side, there in ((0, to_right), (1, to_left)):

            @pl.when(there)
            def _():
                for pair in pairs:
                    pair[side].start()

    def arrived(from_left, from_right, pair, then=None):
        for side, there in ((0, from_left), (1, from_right)):

            @pl.when(there)
            def _():
                pair[side].wait_recv()
                if then:
                    then[side].start()

    def derive(lo, width):
        for q in [lo + i for i in range(width)]:
            d = DT * raw[3, q]
            for axis in range(3):
                v = (0.5 * DT) * raw[axis, q]
                stencil[2 * axis, q] = d - v
                stencil[2 * axis + 1, q] = d + v
            stencil[6, q] = SHIFT - 6.0 * d

    def advance(t, k, lo, width):
        for q in [lo + i for i in range(width)]:
            c = [stencil[j, q - 1] for j in range(7)]
            u = power[k - 1, t, q]
            x = c[0] * power[k - 1, t, q + 1] + c[1] * power[k - 1, t, q - 1]
            y = c[2] * pltpu.roll(u, u.shape[0] - 1, 0) + c[3] * pltpu.roll(u, 1, 0)
            z = c[4] * pltpu.roll(u, u.shape[1] - 1, 1) + c[5] * pltpu.roll(u, 1, 1)
            power[k, t, q] = (x + y) + (z + c[6] * u)

    def accumulate(t, p, lo, hi, before):
        v = [power[k, t, p + EDGE] for k in range(lo, hi)]
        totals = []
        for j in range(SUMS):
            total = before[j] if before else None
            for k in range(lo, hi):
                term = weight[tm, j * (DEGREE + 1) + k] * v[k - lo]
                total = term if total is None else total + term
            totals.append(total)
        return totals

    for copy in loads:
        copy.wait()
    derive(HALO, planes)

    pl.semaphore_wait(barrier, 1 + has_left.astype(jnp.int32) + has_right.astype(jnp.int32))
    start(slow_right, slow_left, near_slow, *first_slow)
    start(fast_right, fast_left, near, *first_round)

    @pl.when(deep_right)
    def _():
        deep[0].start()
        deep_fields[0][0].start()

    for side, there in ((0, deep_right), (1, deep_left)):

        @pl.when(there)
        def _():
            near[side].wait_recv()
            near_pass[side].start()
            if side:
                deep[side].start()
                deep_fields[0][side].start()
            relay[side].start()
            first_round[0][side].wait_recv()
            relay_fields[0][side].start()
            first_round[1][side].wait_recv()
            if not side:
                relay_fields[0][side].wait_send()
                deep_fields[1][side].start()
                relay_fields[1][side].start()

    from_left = jnp.logical_and(fast_left, jnp.logical_not(deep_right))
    from_right = jnp.logical_and(fast_right, jnp.logical_not(deep_left))
    arrived(from_left, from_right, near, near_pass)
    arrived(slow_left, slow_right, near_slow, near_pass_slow)
    start(late_right, late_left, far)
    arrived(fast_left, fast_right, near_pass)
    arrived(slow_left, slow_right, near_pass_slow)
    derive(HALO - S1 + 1, S1 - 1)
    derive(HALO + planes, S1 - 1)

    @pl.when(jnp.logical_not(slow_left))
    def _():
        derive(HALO - NEAR, NEAR - S1 + 1)

    @pl.when(jnp.logical_not(slow_right))
    def _():
        derive(HALO + planes + S1 - 1, NEAR - S1 + 1)

    for t in range(2):
        arrived(from_left, from_right, first_round[t])
        arrived(slow_left, slow_right, first_slow[t])
        for k in range(1, W1 + 1):
            advance(t, k, EDGE - W1 + k, planes + 2 * (W1 - k))
            if k == S1:
                start(late_right, late_left, second_slow[t])
        start(fast_right, fast_left, second_round[t])
        if t == 0:

            @pl.when(deep_left)
            def _():
                deep_fields[1][1].start()
                relay_fields[1][1].start()


    arrived(late_left, late_right, far, far_pass)
    arrived(deep_left, deep_right, deep, deep_pass)
    arrived(deep_left, deep_right, relay, relay_pass)

    for t in range(2):
        for p in range(planes):
            for j, total in enumerate(accumulate(t, p, 0, S1 + 1, None)):
                sums[j, t, p] = total

    for side, late, far_off in ((0, late_left, deep_left), (1, late_right, deep_right)):
        for there, arrivals, width in ((late, [far_pass], S2 - S1), (far_off, [deep_pass, relay_pass], S2)):

            @pl.when(there)
            def _():
                for passes in arrivals:
                    passes[side].wait_recv()
                derive(HALO + planes + S1 - 1 if side else HALO - S1 + 1 - width, width)

    def outer(side, k):
        return EDGE + planes + S1 - k if side else EDGE - DEGREE + k

    def widen(t):
        for side, late, far_off in ((0, late_left, deep_left), (1, late_right, deep_right)):

            @pl.when(far_off)
            def _():
                deep_fields[t][side].wait_recv()
                relay_fields[t][side].wait_recv()
                for i in range(S2):
                    power[0, t, outer(side, 0) + i] = landing[1, t, i]
                for k in range(1, W1 + 1):
                    advance(t, k, outer(side, k), S2)

            @pl.when(late)
            def _():
                second_slow[t][side].wait_recv()
                for i in range(S2):
                    power[S1, t, outer(side, S1) + i] = landing[0, t, i]
                for k in range(S1 + 1, W1 + 1):
                    advance(t, k, outer(side, k), S2)

    crossings = []
    for t in range(2):
        widen(t)
        arrived(fast_left, fast_right, second_round[t])
        for j in range(1, W2 + 1):
            advance(t, W1 + j, EDGE - W2 + j, planes + 2 * (W2 - j))
        for p in range(planes):
            totals = accumulate(t, p, S1 + 1, DEGREE + 1, [sums[j, t, p] for j in range(SUMS)])
            out[2 - 2 * core, first + t, p] = totals[0]
            out[core, first + t, p] = totals[1]
            out[core + 1, first + t, p] = totals[2]
            across[t, 2 * core, p] = totals[0]
            across[t, 1 - core, p] = totals[3]
            across[t, 2 - core, p] = totals[4]
        crossings.append(
            pltpu.make_async_remote_copy(
                src_ref=across.at[t],
                dst_ref=out.at[:, first + t],
                send_sem=cross_send.at[t],
                recv_sem=cross_recv.at[t],
                device_id={"tm": peer},
                device_id_type=MESH,
            )
        )
        crossings[t].start()

    sides = (
        (0, fast_right, slow_right, late_right, deep_right),
        (1, fast_left, slow_left, late_left, deep_left),
    )
    for side, fast, slow, late, far_off in sides:
        for there, copies, passes in (
            (fast, [near, *first_round, *second_round], [near_pass]),
            (slow, [near_slow, *first_slow], [near_pass_slow]),
            (late, [far, *second_slow], [far_pass]),
            (far_off, [deep, relay, *deep_fields, *relay_fields], [deep_pass, relay_pass]),
        ):

            @pl.when(there)
            def _():
                for copy in copies:
                    if side or copy is not relay_fields[0]:
                        copy[side].wait_send()
                for handed in passes:
                    handed[1 - side].wait_send()

    for copy in crossings:
        copy.wait()


def body(initial, velocity, diffusivity):
    planes, rows, lanes = diffusivity.shape
    operands = (jnp.asarray(weights()), initial, velocity, diffusivity)
    nodes = pl.pallas_call(
        functools.partial(kernel, planes),
        out_shape=jax.ShapeDtypeStruct((3,) + initial.shape, jnp.float32),
        in_specs=[pl.BlockSpec(memory_space=pl.ANY)] * 4,
        out_specs=pl.BlockSpec(memory_space=pltpu.VMEM),
        scratch_shapes=[
            pltpu.VMEM((DEGREE + 1, 2, planes + 2 * EDGE, rows, lanes), jnp.float32),
            pltpu.VMEM((4, planes + 2 * HALO, rows, lanes), jnp.float32),
            pltpu.VMEM((7, planes + 2 * HALO, rows, lanes), jnp.float32),
            pltpu.VMEM((SUMS, 2, planes, rows, lanes), jnp.float32),
            pltpu.VMEM((2, 3, planes, rows, lanes), jnp.float32),
            pltpu.VMEM((2, 2, S2, rows, lanes), jnp.float32),
            pltpu.SMEM((SLICES, LANES), jnp.float32),
            pltpu.SemaphoreType.DMA((4,)),
            pltpu.SemaphoreType.DMA((2, 9)),
            pltpu.SemaphoreType.DMA((2, 9)),
            pltpu.SemaphoreType.DMA((3, 2)),
            pltpu.SemaphoreType.DMA((3, 2)),
            pltpu.SemaphoreType.DMA((2,)),
            pltpu.SemaphoreType.DMA((2,)),
        ],
        compiler_params=pltpu.CompilerParams(collective_id=0, has_side_effects=True, vmem_limit_bytes=24 * 2**20),
        name="powers",
    )(*[pltpu.with_memory_space_constraint(a, pltpu.HBM) for a in operands])
    return nodes[None]


def solution(mesh):
    return jax.shard_map(
        body,
        mesh=mesh,
        in_specs=(
            P(None, "space", None, None),
            P(None, "space", None, None),
            P("space", None, None),
        ),
        out_specs=P("tm", None, None, "space", None, None),
        check_vma=False,
    )
```
